256 devices in a mesh: wide: 32 (over x, y, core), narrow: 8 (over z).
Axes of the slice: x: 4, y: 4, z: 8, core: 2. Of those that a mesh axis runs over, the one named last changes fastest.
Arguments:
- events: bfloat16 [32768, 1024], P('wide'), may hold values from -36 to 36
- lengths: int32 [24], replicated, may hold values from 1 to 8192, 32768 in all
- in_gain: float32 [1024], replicated, may hold values from 0.1 to 1.9
- w_uvqk: bfloat16 [1024, 8, 512], P(None, 'narrow'), may hold values from -2 to 2, as said below
- out_gain: float32 [8, 128], P('narrow'), may hold values from 0.1 to 1.9
- w_out: bfloat16 [8, 128, 1024], P('narrow'), may hold values from -0.25 to 0.25
Outputs:
- layer_out: bfloat16 [32768, 1024], P('wide', 'narrow')
The draws below stay inside these ranges and needn't reach their ends.
Inputs may be any that keep to these rules, and one draw needn't show every extreme that they name: `w_uvqk`: projection weights.
All inputs are finite; a program needn't handle non-finite values.
Results may differ from the reference program's by a relative error of at most 0.0036.
Values may be sent and summed in bfloat16 or wider, within the bound.
No kernel may reach another device: no remote copies, remote signals or barrier semaphores. Data moves between devices by JAX's collectives and lax.ppermute only.
A program may use at most 64 MiB of HBM per device.

```python
import math
import jax
import jax.numpy as jnp
import numpy as np
from jax import lax

D = 1024
H = 8
DH = 128
USERS = 24
ROWS_W = 1024
TOTAL = 32768
MOST = 8192


def draw_events(key, part):
    key_rows, key_cols, key_dirs, key_offsets, key_spread, key_noise = jax.random.split(jax.random.fold_in(key, 7), 6)
    row_scale = jnp.exp(jax.random.uniform(key_rows, (TOTAL, 1), jnp.float32, jnp.log(0.3), jnp.log(3.0)))
    col_scale = jnp.exp(jax.random.uniform(key_cols, (1, D), jnp.float32, jnp.log(0.3), jnp.log(3.0)))
    segment_len = max(ROWS_W * 3 // 8, 1)
    segment_count = TOTAL // segment_len + 1
    segment_of = (jnp.arange(TOTAL, dtype=jnp.int32) // segment_len).astype(jnp.int32)
    directions = jnp.clip(jax.random.normal(key_dirs, (3, D), jnp.float32), -3.0, 3.0)
    offsets = 0.6 * jnp.clip(jax.random.normal(key_offsets, (segment_count, 3), jnp.float32), -3.0, 3.0)
    spread = 0.45 * jnp.clip(jax.random.normal(key_spread, (TOTAL, 3), jnp.float32), -3.0, 3.0)
    noise = 0.6 * jnp.clip(jax.random.normal(key_noise, (TOTAL, D), jnp.float32), -4.0, 4.0)
    coefficients = jnp.take(offsets, segment_of, axis=0) + spread
    inner = coefficients[:, 0:1] * directions[0:1] + coefficients[:, 1:2] * directions[1:2]
    inner = inner + coefficients[:, 2:3] * directions[2:3] + noise
    inner = jnp.clip(inner, -4.0, 4.0)
    return (inner * row_scale * col_scale).astype(jnp.bfloat16)


def draw_w_uvqk(key, part):
    key_base, key_own = jax.random.split(jax.random.fold_in(key, 11), 2)
    base = jnp.clip(jax.random.normal(key_base, (D, H, 4 * DH), jnp.float32), -5.0, 5.0)
    own = jnp.clip(jax.random.normal(key_own, (D, H, DH), jnp.float32), -5.0, 5.0)
    narrow_scale = D ** (-0.5)
    broad_scale = (3.0 / D) ** 0.5
    gate_value = base[:, :, :2 * DH] * narrow_scale
    query_part = base[:, :, 2 * DH:3 * DH]
    key_part = 0.9 * query_part + 0.44 * own
    whole = jnp.concatenate([gate_value, query_part * broad_scale, key_part * broad_scale], axis=2)
    return whole.astype(jnp.bfloat16)


def with_spikes(array, rng, source, target, blocks, factor):
    owner, partner = [(jnp.arange(array.shape[position]) // (array.shape[position] // blocks)).reshape([-1 if axis == position else 1 for axis in range(array.ndim)]) for position in (source, target)]
    chosen = jax.random.permutation(rng, blocks)[partner]
    strong = (owner == chosen) | (owner == (partner + blocks // 2) % blocks)
    return jnp.where(strong, factor * array, array)


def shard_levels(stream_key, extent, cuts, low, top_value):
    factor_of = 1.0
    for axis_at, shards_of in cuts:
        steps = jax.random.uniform(jax.random.fold_in(jax.random.fold_in(stream_key, 6), axis_at), (shards_of,), jnp.float32, low / len(cuts), top_value / len(cuts))
        factor_of = factor_of * jnp.repeat(jnp.exp(steps), extent[axis_at] // shards_of).reshape((-1,) + (1,) * (len(extent) - 1 - axis_at))
    return factor_of


def profile(count, total, bound, lean):
    loads = [(1 << 20) // math.isqrt(grade ** lean) + 1 for grade in range(2, count + 1)]
    spare, given = total - bound - (count - 1), [1] * (count - 1)
    while spare > 0:
        movable = [i for i in range(count - 1) if given[i] < bound]
        mass, budget = sum([loads[i] for i in movable]), spare
        for i in movable:
            more = min(bound - given[i], max(1, budget * loads[i] // mass), spare)
            given[i] = given[i] + more
            spare = spare - more
    return np.array([bound] + given)


def ragged_sizes(key, amount, total, limit, skew):
    if amount == 2:
        one = jax.random.randint(key, (), max(1, total - limit), min(limit, total - 1) + 1)
        return jnp.stack([one, total - one])
    tallies = jnp.asarray(profile(amount, total, limit, skew), jnp.int32)
    couples = (amount - 1) // 2
    donor, receiver = tallies[1:1 + 2 * couples:2], tallies[2:2 + 2 * couples:2]
    slack = jnp.minimum(donor - 1, limit - receiver)
    passed = jax.random.randint(jax.random.fold_in(key, 1), (couples,), 0, 1 << 20) % (slack + 1)
    tallies = tallies.at[1:1 + 2 * couples:2].set(donor - passed).at[2:2 + 2 * couples:2].set(receiver + passed)
    return tallies[jax.random.permutation(jax.random.fold_in(key, 2), amount)]


def noise_with(stream_key, extent, scale, limit, cuts, heavy, kind=jnp.bfloat16):
    values = scale * jax.random.normal(stream_key, extent, jnp.float32)
    if cuts:
        values = values * shard_levels(stream_key, extent, cuts, -0.22, 0.18)
    return jnp.clip(with_spikes(values, jax.random.fold_in(stream_key, 3), *heavy), -limit, limit).astype(kind)


def setup_inputs(seed: int = 0) -> dict:
    streams_of = jax.random.split(jax.random.key(seed), 7)
    return {
        "events": draw_events(jax.random.fold_in(streams_of[6], 71), 0),
        "lengths": ragged_sizes(streams_of[1], USERS, TOTAL, MOST, 2).astype(jnp.int32),
        "in_gain": jnp.clip(1.0 + 0.18 * jax.random.normal(streams_of[2], (D,), jnp.float32), 0.1, 1.9),
        "w_uvqk": draw_w_uvqk(jax.random.fold_in(streams_of[6], 71), 0),
        "out_gain": jnp.clip(1.0 + 0.18 * jax.random.normal(streams_of[4], (H, DH), jnp.float32), 0.1, 1.9),
        "w_out": noise_with(streams_of[5], (H, DH, D), (H * DH) ** -0.5, 0.25, ((0, 8),), (0, 2, 8, 2.0)),
    }


def reference(events, lengths, in_gain, w_uvqk, out_gain, w_out):
    events_f = events.astype(jnp.float32)
    average = lax.optimization_barrier(jnp.mean(events_f, axis=-1, keepdims=True))
    variance = lax.optimization_barrier(jnp.mean((events_f - average) ** 2, axis=-1, keepdims=True))
    normed = ((events_f - average) * lax.rsqrt(variance + 1e-05) * in_gain).astype(jnp.bfloat16)
    projected = jnp.dot(normed, w_uvqk.reshape(D, H * 4 * DH), preferred_element_type=jnp.float32)
    projected = jax.nn.silu(projected).reshape(TOTAL, H, 4 * DH).astype(jnp.bfloat16)
    update_gate = projected[:, :, :DH]
    values_all = projected[:, :, DH:2 * DH]
    queries = projected[:, :, 2 * DH:3 * DH]
    keys_all = projected[:, :, 3 * DH:]
    user_ends = jnp.cumsum(lengths).astype(jnp.int32)
    positions = jnp.arange(TOTAL, dtype=jnp.int32)
    owners = lax.optimization_barrier(jnp.sum((user_ends[None, :] <= positions[:, None]).astype(jnp.int32), axis=1))
    query_rows = min(512, TOTAL)
    window = min(TOTAL, MOST + query_rows)
    scaling = DH ** (-0.5)

    def query_block(block_index):
        query_start = block_index * query_rows
        key_start = jnp.clip(query_start + query_rows - window, 0, TOTAL - window).astype(jnp.int32)
        query_part = lax.dynamic_slice_in_dim(queries, query_start, query_rows, 0).astype(jnp.float32)
        query_pos = lax.dynamic_slice_in_dim(positions, query_start, query_rows, 0)
        query_user = lax.dynamic_slice_in_dim(owners, query_start, query_rows, 0)
        key_part = lax.dynamic_slice_in_dim(keys_all, key_start, window, 0).astype(jnp.float32)
        value_part = lax.dynamic_slice_in_dim(values_all, key_start, window, 0).astype(jnp.float32)
        key_pos = lax.dynamic_slice_in_dim(positions, key_start, window, 0)
        key_user = lax.dynamic_slice_in_dim(owners, key_start, window, 0)
        scores = jnp.einsum('rhc,khc->hrk', query_part, key_part) * scaling
        allowed = (key_user[None, :] == query_user[:, None]) & (key_pos[None, :] <= query_pos[:, None])
        weights = jnp.where(allowed[None], jax.nn.silu(scores), 0.0).astype(jnp.bfloat16)
        return jnp.einsum('hrk,khc->rhc', weights.astype(jnp.float32), value_part)
    attended = lax.map(query_block, jnp.arange(TOTAL // query_rows, dtype=jnp.int32))
    attended = attended.reshape(TOTAL, H, DH)
    centre = lax.optimization_barrier(jnp.mean(attended, axis=-1, keepdims=True))
    deviation = lax.optimization_barrier(jnp.mean((attended - centre) ** 2, axis=-1, keepdims=True))
    gated = (attended - centre) * lax.rsqrt(deviation + 1e-05) * out_gain[None] * update_gate.astype(jnp.float32)
    gated = gated.astype(jnp.bfloat16)
    branch = jnp.dot(gated.reshape(TOTAL, H * DH), w_out.reshape(H * DH, D), preferred_element_type=jnp.float32)
    return (events_f + branch).astype(jnp.bfloat16)
```

```python
import functools

import jax
import jax.numpy as jnp
from jax import lax
from jax.experimental import pallas as pl
from jax.experimental.pallas import tpu as pltpu
from jax.sharding import PartitionSpec as P

F32 = jnp.float32
BF16 = jnp.bfloat16
SMEM = pl.BlockSpec(memory_space=pltpu.SMEM)
VMEM = pl.BlockSpec(memory_space=pltpu.VMEM)
ROWS = 1024
DH = 128
TQ = 512
TK = 256
NT = (((1,), (1,)), ((), ()))


def silu(x):
    half = 0.5 * x
    return half + half * jnp.tanh(half)


def project_kernel(events_ref, gain_ref, w_ref, kv_ref, q_ref, u_ref):
    x = events_ref[...].astype(F32)
    average = jnp.mean(x, axis=-1, keepdims=True)
    centred = x - average
    variance = jnp.mean(centred * centred, axis=-1, keepdims=True)
    normed = (centred * lax.rsqrt(variance + 1e-05) * gain_ref[...]).astype(BF16)
    out = silu(jnp.dot(normed, w_ref[...], preferred_element_type=F32)).astype(BF16)
    u_ref[...] = out[:, :DH]
    q_ref[...] = out[:, 2 * DH : 3 * DH]
    kv_ref[:, :DH] = out[:, 3 * DH :]
    kv_ref[:, DH:] = out[:, DH : 2 * DH]


def project(events, in_gain, w):
    rows, width = events.shape
    tile = 256
    return pl.pallas_call(
        project_kernel,
        grid=(rows // tile,),
        in_specs=[
            pl.BlockSpec((tile, width), lambda i: (i, 0)),
            pl.BlockSpec((1, width), lambda i: (0, 0)),
            pl.BlockSpec((width, 4 * DH), lambda i: (0, 0)),
        ],
        out_specs=[
            pl.BlockSpec((tile, 2 * DH), lambda i: (i, 0)),
            pl.BlockSpec((tile, DH), lambda i: (i, 0)),
            pl.BlockSpec((tile, DH), lambda i: (i, 0)),
        ],
        out_shape=[
            jax.ShapeDtypeStruct((rows, 2 * DH), BF16),
            jax.ShapeDtypeStruct((rows, DH), BF16),
            jax.ShapeDtypeStruct((rows, DH), BF16),
        ],
        cost_estimate=pl.CostEstimate(
            flops=2 * rows * width * 4 * DH, bytes_accessed=4 << 20, transcendentals=rows * 4 * DH
        ),
        name="project",
    )(events, in_gain[None], w)


def attend_kernel(users, count, first, ends_ref, base_ref, *refs):
    starts_ref, q_own, q_sib = refs[:3]
    blocks = refs[3 : 3 + count]
    carried = refs[3 + count : -2]
    outs = refs[-2:]
    scale = 0.5 * DH ** (-0.5)

    def weigh(scores):
        half = scores * scale
        return half + half * jnp.tanh(half)

    for side, q_ref in enumerate((q_own, q_sib)):
        out_ref = outs[side]
        if first:
            out_ref[...] = jnp.zeros_like(out_ref)
        else:
            out_ref[...] = carried[side][...]
        for part in range(ROWS // TQ):
            q_first = base_ref[side] + part * TQ
            q_last = q_first + TQ - 1
            low = jnp.int32(0)
            high = jnp.int32(0)
            for user in range(users):
                end = ends_ref[user]
                low = jnp.where(end <= q_first, end, low)
                high = jnp.where(end <= q_last, end, high)
            rows = pl.ds(part * TQ, TQ)
            for index, kv_ref in enumerate(blocks):
                k_first = base_ref[2 + index]
                reached = (k_first >= 0) & (k_first + ROWS > low) & (k_first <= q_last)
                whole = (k_first >= high) & (k_first + ROWS - 1 <= q_first)

                @pl.when(reached & whole)
                def _():
                    total = out_ref[rows, :]
                    q = q_ref[rows, :]
                    for piece in range(ROWS // TK):
                        keys = kv_ref[piece * TK : (piece + 1) * TK, :DH]
                        values = kv_ref[piece * TK : (piece + 1) * TK, DH:]
                        scores = lax.dot_general(q, keys, NT, preferred_element_type=F32)
                        total += jnp.dot(weigh(scores).astype(BF16), values, preferred_element_type=F32)
                    out_ref[rows, :] = total

                @pl.when(reached & jnp.logical_not(whole))
                def _():
                    q = q_ref[rows, :]
                    begin = jnp.maximum(low - k_first, 0) // TK
                    stop = jnp.minimum((q_last - k_first) // TK + 1, ROWS // TK)
                    q_start = starts_ref[pl.ds(side * ROWS + part * TQ, TQ), :]
                    q_pos = q_first + lax.broadcasted_iota(jnp.int32, (TQ, DH), 0)

                    def step(piece, carry):
                        at = pl.multiple_of(piece * TK, TK)
                        keys = kv_ref[pl.ds(at, TK), :DH]
                        values = kv_ref[pl.ds(at, TK), DH:]
                        scores = lax.dot_general(q, keys, NT, preferred_element_type=F32)
                        lanes = lax.broadcasted_iota(jnp.int32, (TQ, DH), 1) + (k_first + at)
                        allowed = []
                        for strip in range(TK // DH):
                            k_pos = lanes + strip * DH
                            keep = (k_pos >= q_start) & (k_pos <= q_pos)
                            allowed.append(
                                jnp.where(keep, weigh(scores[:, strip * DH : (strip + 1) * DH]), 0.0)
                            )
                        weights = jnp.concatenate(allowed, axis=1).astype(BF16)
                        out_ref[rows, :] += jnp.dot(weights, values, preferred_element_type=F32)
                        return carry

                    lax.fori_loop(begin, stop, step, 0)


def attend(ends, bases, starts, q_own, q_sib, blocks, carried=None):
    count = len(blocks)
    first = carried is None
    carried = () if first else tuple(carried)
    return pl.pallas_call(
        functools.partial(attend_kernel, ends.shape[0], count, first),
        in_specs=[SMEM, SMEM] + [VMEM] * (3 + count + len(carried)),
        out_specs=[VMEM, VMEM],
        out_shape=[jax.ShapeDtypeStruct((ROWS, DH), F32)] * 2,
        input_output_aliases={} if first else {5 + count: 0, 6 + count: 1},
        compiler_params=pltpu.CompilerParams(vmem_limit_bytes=40 << 20),
        cost_estimate=pl.CostEstimate(
            flops=count * 8 * ROWS * ROWS * DH,
            bytes_accessed=(2 + count) << 19,
            transcendentals=count * 2 * ROWS * ROWS,
        ),
        name="attend",
    )(ends, bases, starts, q_own, q_sib, *blocks, *carried)


def gate_kernel(own_ref, sib_ref, u_ref, gain_ref, out_ref):
    attended = own_ref[...] + sib_ref[...]
    centre = jnp.mean(attended, axis=-1, keepdims=True)
    centred = attended - centre
    deviation = jnp.mean(centred * centred, axis=-1, keepdims=True)
    gated = centred * lax.rsqrt(deviation + 1e-05) * gain_ref[...] * u_ref[...].astype(F32)
    out_ref[...] = gated.astype(BF16)


def gate(own, sib, u, gain):
    return pl.pallas_call(
        gate_kernel,
        in_specs=[VMEM] * 4,
        out_specs=VMEM,
        out_shape=jax.ShapeDtypeStruct(u.shape, BF16),
        name="gate",
    )(own, sib, u, gain)


def combine_kernel(heads, gated_ref, w_ref, events_ref, out_ref):
    gated = jnp.concatenate([gated_ref[head] for head in range(heads)], axis=1)
    total = jnp.dot(gated, w_ref[...], preferred_element_type=F32)
    total = (total + events_ref[...].astype(F32)).astype(BF16)
    for head in range(heads):
        out_ref[head] = total[:, head * DH : (head + 1) * DH]


def combine(gated, w, events):
    heads = gated.shape[0]
    return pl.pallas_call(
        functools.partial(combine_kernel, heads),
        in_specs=[VMEM] * 3,
        out_specs=VMEM,
        out_shape=jax.ShapeDtypeStruct(gated.shape, BF16),
        name="combine",
    )(gated, w, events)


def on_device(events, lengths, in_gain, w_uvqk, out_gain, w_out):
    rows, width = events.shape
    heads = lax.axis_size("narrow")
    count = lax.axis_size("wide")
    me = lax.axis_index("wide")
    chip, core = me // 2, me % 2

    def moved(value, steps):
        return lax.ppermute(value, "wide", [(i, (i + steps) % count) for i in range(count)])

    def swapped(value):
        return lax.ppermute(value, "wide", [(i, i ^ 1) for i in range(count)])

    w_all = lax.all_gather(w_out[0], "narrow", axis=0, tiled=True)
    kv, q, u = project(events, in_gain, w_uvqk[:, 0, :])

    users = lengths.shape[0]
    upto = jnp.arange(users)[:, None] >= jnp.arange(users)[None, :]
    ends = jnp.sum(jnp.where(upto, lengths[None, :], 0), axis=1)
    both = jnp.concatenate([me * rows + jnp.arange(rows), (me ^ 1) * rows + jnp.arange(rows)])
    starts = jnp.max(jnp.where(ends[None, :] <= both[:, None], ends[None, :], 0), axis=1)
    starts = jnp.broadcast_to(starts[:, None], (2 * rows, DH)).astype(jnp.int32)

    def bases(*back):
        return jnp.stack([me * rows, (me ^ 1) * rows] + [(me - 2 * d) * rows for d in back]).astype(jnp.int32)

    q_sib = swapped(q)
    kv1 = moved(kv, 2)
    kv4 = moved(kv, 8)
    kv2 = moved(kv1, 2)
    kv3 = moved(kv4, -2)
    acc = attend(ends, bases(0), starts, q, q_sib, [kv])
    acc = attend(ends, bases(1, 4), starts, q, q_sib, [kv1, kv4], acc)
    own, sib = attend(ends, bases(2, 3), starts, q, q_sib, [kv2, kv3], acc)
    gated = gate(own, swapped(sib), u, out_gain)
    share = rows // heads
    gated = lax.all_to_all(gated.reshape(heads, share, DH), "narrow", 0, 0)
    mine = lax.dynamic_slice_in_dim(events, lax.axis_index("narrow") * share, share, 0)
    out = combine(gated, w_all, mine)
    return lax.all_to_all(out, "narrow", 0, 0).reshape(rows, DH)


def solution(mesh):
    in_specs = (
        P("wide", None),
        P(),
        P(),
        P(None, "narrow", None),
        P("narrow", None),
        P("narrow", None, None),
    )
    out_specs = P("wide", "narrow")
    return jax.shard_map(
        on_device, mesh=mesh, in_specs=in_specs, out_specs=out_specs, check_vma=False
    )
```

```python
import functools

import jax
import jax.numpy as jnp
from jax import lax
from jax.experimental import pallas as pl
from jax.experimental.pallas import tpu as pltpu
from jax.sharding import PartitionSpec as P

F32 = jnp.float32
BF16 = jnp.bfloat16
SMEM = pl.BlockSpec(memory_space=pltpu.SMEM)
VMEM = pl.BlockSpec(memory_space=pltpu.VMEM)
ROWS = 1024
DH = 128
TQ = 512
TK = 256
NT = (((1,), (1,)), ((), ()))


def silu(x):
    half = 0.5 * x
    return half + half * jnp.tanh(half)


def project_kernel(events_ref, gain_ref, w_ref, kv_ref, q_ref, u_ref):
    x = events_ref[...].astype(F32)
    average = jnp.mean(x, axis=-1, keepdims=True)
    centred = x - average
    variance = jnp.mean(centred * centred, axis=-1, keepdims=True)
    normed = (centred * lax.rsqrt(variance + 1e-05) * gain_ref[...]).astype(BF16)
    out = silu(jnp.dot(normed, w_ref[...], preferred_element_type=F32)).astype(BF16)
    u_ref[...] = out[:, :DH]
    q_ref[...] = out[:, 2 * DH : 3 * DH]
    kv_ref[:, :DH] = out[:, 3 * DH :]
    kv_ref[:, DH:] = out[:, DH : 2 * DH]


def project(events, in_gain, w):
    rows, width = events.shape
    tile = 256
    return pl.pallas_call(
        project_kernel,
        grid=(rows // tile,),
        in_specs=[
            pl.BlockSpec((tile, width), lambda i: (i, 0)),
            pl.BlockSpec((1, width), lambda i: (0, 0)),
            pl.BlockSpec((width, 4 * DH), lambda i: (0, 0)),
        ],
        out_specs=[
            pl.BlockSpec((tile, 2 * DH), lambda i: (i, 0)),
            pl.BlockSpec((tile, DH), lambda i: (i, 0)),
            pl.BlockSpec((tile, DH), lambda i: (i, 0)),
        ],
        out_shape=[
            jax.ShapeDtypeStruct((rows, 2 * DH), BF16),
            jax.ShapeDtypeStruct((rows, DH), BF16),
            jax.ShapeDtypeStruct((rows, DH), BF16),
        ],
        cost_estimate=pl.CostEstimate(
            flops=2 * rows * width * 4 * DH, bytes_accessed=4 << 20, transcendentals=rows * 4 * DH
        ),
        compiler_params=pltpu.CompilerParams(vmem_limit_bytes=12 << 20),
        name="project",
    )(events, in_gain[None], w)


def attend_kernel(users, count, first, ends_ref, base_ref, *refs):
    starts_ref, q_own, q_sib = refs[:3]
    blocks = refs[3 : 3 + count]
    carried = refs[3 + count : -2]
    outs = refs[-2:]
    scale = 0.5 * DH ** (-0.5)

    def weigh(scores):
        half = scores * scale
        return half + half * jnp.tanh(half)

    for side, q_ref in enumerate((q_own, q_sib)):
        out_ref = outs[side]
        if first:
            out_ref[...] = jnp.zeros_like(out_ref)
        else:
            out_ref[...] = carried[side][...]
        for part in range(ROWS // TQ):
            q_first = base_ref[side] + part * TQ
            q_last = q_first + TQ - 1
            low = jnp.int32(0)
            high = jnp.int32(0)
            for user in range(users):
                end = ends_ref[user]
                low = jnp.where(end <= q_first, end, low)
                high = jnp.where(end <= q_last, end, high)
            rows = pl.ds(part * TQ, TQ)
            for index, kv_ref in enumerate(blocks):
                k_first = base_ref[2 + index]
                reached = (k_first >= 0) & (k_first + ROWS > low) & (k_first <= q_last)
                whole = (k_first >= high) & (k_first + ROWS - 1 <= q_first)

                @pl.when(reached & whole)
                def _():
                    total = out_ref[rows, :]
                    q = q_ref[rows, :]
                    for piece in range(ROWS // TK):
                        keys = kv_ref[piece * TK : (piece + 1) * TK, :DH]
                        values = kv_ref[piece * TK : (piece + 1) * TK, DH:]
                        scores = lax.dot_general(q, keys, NT, preferred_element_type=F32)
                        total += jnp.dot(weigh(scores).astype(BF16), values, preferred_element_type=F32)
                    out_ref[rows, :] = total

                @pl.when(reached & jnp.logical_not(whole))
                def _():
                    q = q_ref[rows, :]
                    begin = jnp.maximum(low - k_first, 0) // TK
                    stop = jnp.minimum((q_last - k_first) // TK + 1, ROWS // TK)
                    q_start = starts_ref[pl.ds(side * ROWS + part * TQ, TQ), :]
                    q_pos = q_first + lax.broadcasted_iota(jnp.int32, (TQ, DH), 0)

                    def step(piece, carry):
                        at = pl.multiple_of(piece * TK, TK)
                        keys = kv_ref[pl.ds(at, TK), :DH]
                        values = kv_ref[pl.ds(at, TK), DH:]
                        scores = lax.dot_general(q, keys, NT, preferred_element_type=F32)
                        lanes = lax.broadcasted_iota(jnp.int32, (TQ, DH), 1) + (k_first + at)
                        allowed = []
                        for strip in range(TK // DH):
                            k_pos = lanes + strip * DH
                            keep = (k_pos >= q_start) & (k_pos <= q_pos)
                            allowed.append(
                                jnp.where(keep, weigh(scores[:, strip * DH : (strip + 1) * DH]), 0.0)
                            )
                        weights = jnp.concatenate(allowed, axis=1).astype(BF16)
                        out_ref[rows, :] += jnp.dot(weights, values, preferred_element_type=F32)
                        return carry

                    lax.fori_loop(begin, stop, step, 0)


def attend(ends, bases, starts, q_own, q_sib, blocks, carried=None):
    count = len(blocks)
    first = carried is None
    carried = () if first else tuple(carried)
    return pl.pallas_call(
        functools.partial(attend_kernel, ends.shape[0], count, first),
        in_specs=[SMEM, SMEM] + [VMEM] * (3 + count + len(carried)),
        out_specs=[VMEM, VMEM],
        out_shape=[jax.ShapeDtypeStruct((ROWS, DH), F32)] * 2,
        input_output_aliases={} if first else {5 + count: 0, 6 + count: 1},
        compiler_params=pltpu.CompilerParams(vmem_limit_bytes=24 << 20),
        cost_estimate=pl.CostEstimate(
            flops=count * 8 * ROWS * ROWS * DH,
            bytes_accessed=(2 + count) << 19,
            transcendentals=count * 2 * ROWS * ROWS,
        ),
        name="attend",
    )(ends, bases, starts, q_own, q_sib, *blocks, *carried)


def gate_kernel(own_ref, sib_ref, u_ref, gain_ref, out_ref):
    attended = own_ref[...] + sib_ref[...]
    centre = jnp.mean(attended, axis=-1, keepdims=True)
    centred = attended - centre
    deviation = jnp.mean(centred * centred, axis=-1, keepdims=True)
    gated = centred * lax.rsqrt(deviation + 1e-05) * gain_ref[...] * u_ref[...].astype(F32)
    out_ref[...] = gated.astype(BF16)


def gate(own, sib, u, gain):
    return pl.pallas_call(
        gate_kernel,
        in_specs=[VMEM] * 4,
        out_specs=VMEM,
        out_shape=jax.ShapeDtypeStruct(u.shape, BF16),
        compiler_params=pltpu.CompilerParams(vmem_limit_bytes=8 << 20),
        name="gate",
    )(own, sib, u, gain)


def combine_kernel(heads, gated_ref, w_ref, events_ref, out_ref):
    gated = jnp.concatenate([gated_ref[head] for head in range(heads)], axis=1)
    total = jnp.dot(gated, w_ref[...], preferred_element_type=F32)
    total = (total + events_ref[...].astype(F32)).astype(BF16)
    for head in range(heads):
        out_ref[head] = total[:, head * DH : (head + 1) * DH]


def combine(gated, w, events):
    heads = gated.shape[0]
    return pl.pallas_call(
        functools.partial(combine_kernel, heads),
        in_specs=[VMEM] * 3,
        out_specs=VMEM,
        out_shape=jax.ShapeDtypeStruct(gated.shape, BF16),
        compiler_params=pltpu.CompilerParams(vmem_limit_bytes=8 << 20),
        name="combine",
    )(gated, w, events)


def on_device(events, lengths, in_gain, w_uvqk, out_gain, w_out):
    rows, width = events.shape
    heads = lax.axis_size("narrow")
    count = lax.axis_size("wide")
    me = lax.axis_index("wide")
    chip, core = me // 2, me % 2

    def moved(value, steps):
        return lax.ppermute(value, "wide", [(i, (i + steps) % count) for i in range(count)])

    def swapped(value):
        return lax.ppermute(value, "wide", [(i, i ^ 1) for i in range(count)])

    w_all = lax.all_gather(w_out[0], "narrow", axis=0, tiled=True)
    kv, q, u = project(events, in_gain, w_uvqk[:, 0, :])

    users = lengths.shape[0]
    upto = jnp.arange(users)[:, None] >= jnp.arange(users)[None, :]
    ends = jnp.sum(jnp.where(upto, lengths[None, :], 0), axis=1)
    both = jnp.concatenate([me * rows + jnp.arange(rows), (me ^ 1) * rows + jnp.arange(rows)])
    starts = jnp.max(jnp.where(ends[None, :] <= both[:, None], ends[None, :], 0), axis=1)
    starts = jnp.broadcast_to(starts[:, None], (2 * rows, DH)).astype(jnp.int32)

    def bases(*back):
        return jnp.stack([me * rows, (me ^ 1) * rows] + [(me - 2 * d) * rows for d in back]).astype(jnp.int32)

    q_sib = swapped(q)
    kv1 = moved(kv, 2)
    kv4 = moved(kv, 8)
    acc = attend(ends, bases(0), starts, q, q_sib, [kv])
    kv1, kv4, acc = lax.optimization_barrier((kv1, kv4, acc))
    kv2 = moved(kv1, 2)
    kv3 = moved(kv4, -2)
    acc = attend(ends, bases(1, 4), starts, q, q_sib, [kv1, kv4], acc)
    own, sib = attend(ends, bases(2, 3), starts, q, q_sib, [kv2, kv3], acc)
    gated = gate(own, swapped(sib), u, out_gain)
    share = rows // heads
    gated = lax.all_to_all(gated.reshape(heads, share, DH), "narrow", 0, 0)
    mine = lax.dynamic_slice_in_dim(events, lax.axis_index("narrow") * share, share, 0)
    out = combine(gated, w_all, mine)
    return lax.all_to_all(out, "narrow", 0, 0).reshape(rows, DH)


def solution(mesh):
    in_specs = (
        P("wide", None),
        P(),
        P(),
        P(None, "narrow", None),
        P("narrow", None),
        P("narrow", None, None),
    )
    out_specs = P("wide", "narrow")
    return jax.shard_map(
        on_device, mesh=mesh, in_specs=in_specs, out_specs=out_specs, check_vma=False
    )
```

```python
import functools

import jax
import jax.numpy as jnp
from jax import lax
from jax.experimental import pallas as pl
from jax.experimental.pallas import tpu as pltpu
from jax.sharding import PartitionSpec as P

F32 = jnp.float32
BF16 = jnp.bfloat16
SMEM = pl.BlockSpec(memory_space=pltpu.SMEM)
VMEM = pl.BlockSpec(memory_space=pltpu.VMEM)
ROWS = 1024
DH = 128
HALF = 512
TQ = 512
TK = 256
NT = (((1,), (1,)), ((), ()))


def silu(x):
    half = 0.5 * x
    return half + half * jnp.tanh(half)


def kept(*values):
    return [pltpu.with_memory_space_constraint(value, pltpu.VMEM) for value in values]


def project_kernel(
    parts, events_hbm, gain_ref, w_hbm, kv_ref, kva_ref, kvb_ref, q_ref, u_ref, events, w, sems
):
    rows = events.shape[0] // parts
    fetch_w = pltpu.make_async_copy(w_hbm, w, sems.at[parts])
    fetches = [
        pltpu.make_async_copy(
            events_hbm.at[pl.ds(part * rows, rows)], events.at[pl.ds(part * rows, rows)], sems.at[part]
        )
        for part in range(parts)
    ]
    fetches[0].start()
    fetch_w.start()
    for fetch in fetches[1:]:
        fetch.start()
    for part in range(parts):
        fetches[part].wait()
        x = events[part * rows : (part + 1) * rows, :].astype(F32)
        average = jnp.mean(x, axis=-1, keepdims=True)
        centred = x - average
        variance = jnp.mean(centred * centred, axis=-1, keepdims=True)
        normed = (centred * lax.rsqrt(variance + 1e-05) * gain_ref[...]).astype(BF16)
        if part == 0:
            fetch_w.wait()
        out = silu(jnp.dot(normed, w[...], preferred_element_type=F32)).astype(BF16)
        at = slice(part * rows, (part + 1) * rows)
        u_ref[at, :] = out[:, :DH]
        q_ref[at, :] = out[:, 2 * DH : 3 * DH]
        keys, values = out[:, 3 * DH :], out[:, DH : 2 * DH]
        kv_ref[at, :DH] = keys
        kv_ref[at, DH:] = values
        half_ref = kva_ref if part * rows < HALF else kvb_ref
        at = slice(part * rows % HALF, part * rows % HALF + rows)
        half_ref[at, :DH] = keys
        half_ref[at, DH:] = values


def project(events, in_gain, w):
    rows, width = events.shape
    parts = 4
    hbm = pl.BlockSpec(memory_space=pltpu.HBM)
    return pl.pallas_call(
        functools.partial(project_kernel, parts),
        in_specs=[hbm, VMEM, hbm],
        out_specs=[VMEM] * 5,
        out_shape=[
            pltpu.VMEM((rows, 2 * DH), BF16),
            pltpu.VMEM((HALF, 2 * DH), BF16),
            pltpu.VMEM((HALF, 2 * DH), BF16),
            pltpu.VMEM((rows, DH), BF16),
            pltpu.VMEM((rows, DH), BF16),
        ],
        scratch_shapes=[
            pltpu.VMEM((rows, width), BF16),
            pltpu.VMEM((width, 4 * DH), BF16),
            pltpu.SemaphoreType.DMA((parts + 1,)),
        ],
        cost_estimate=pl.CostEstimate(
            flops=2 * rows * width * 4 * DH, bytes_accessed=4 << 20, transcendentals=rows * 4 * DH
        ),
        compiler_params=pltpu.CompilerParams(vmem_limit_bytes=20 << 20),
        name="project",
    )(
        pltpu.with_memory_space_constraint(events, pltpu.HBM),
        in_gain[None],
        pltpu.with_memory_space_constraint(w, pltpu.HBM),
    )


def attend_kernel(users, pieces, count, first, last, place_ref, lengths_ref, q_own, q_sib, *refs):
    blocks, refs = refs[:count], refs[count:]
    if first:
        outs, starts_ref, q_ref, total_ref = refs[:1], *refs[1:]
    else:
        starts_ref, carried = refs[:2]
        outs, (q_ref, total_ref) = refs[2:-2], refs[-2:]
    me = place_ref[0]
    corner = me // 2 % 4
    scale = 0.5 * DH ** (-0.5)

    def weigh(scores):
        half = scores * scale
        return half + half * jnp.tanh(half)

    q_ref[:ROWS, :] = q_own[...]
    q_ref[ROWS:, :] = q_sib[...]
    if first:
        total_ref[...] = jnp.zeros_like(total_ref)
    else:
        total_ref[...] = carried[...]

    def one_part(part, nothing):
        side, inner = part // (ROWS // TQ), part % (ROWS // TQ)
        q_first = jnp.where(side == 0, me, me + 1 - 2 * (me % 2)) * ROWS + inner * TQ
        q_last = q_first + TQ - 1
        rows = pl.ds(pl.multiple_of(part * TQ, TQ), TQ)
        end = jnp.int32(0)
        low = jnp.int32(0)
        high = jnp.int32(0)
        for user in range(users):
            end = end + lengths_ref[user]
            low = jnp.where(end <= q_first, end, low)
            high = jnp.where(end <= q_last, end, high)
        if first:
            starts_ref[rows, :] = jnp.full((TQ, DH), low, jnp.int32)
            end = jnp.int32(0)
            for user in range(users):
                end = end + lengths_ref[user]

                @pl.when((end > q_first) & (end <= q_last))
                def _(end=end):
                    after = q_first + lax.broadcasted_iota(jnp.int32, (TQ, DH), 0) >= end
                    starts_ref[rows, :] = jnp.where(after, end, starts_ref[rows, :])

        for block, offset, back, corners, shift in pieces:
            kv_ref = blocks[block]
            k_first = (me - back) * ROWS + shift + offset
            held = functools.reduce(jnp.logical_or, [corner == c for c in corners])
            reached = held & (me >= back) & (k_first + HALF > low) & (k_first <= q_last)
            whole = (k_first >= high) & (k_first + HALF - 1 <= q_first)

            @pl.when(reached & whole)
            def _():
                q = q_ref[rows, :]
                weights = []
                for piece in range(HALF // TK):
                    keys = kv_ref[offset + piece * TK : offset + (piece + 1) * TK, :DH]
                    scores = lax.dot_general(q, keys, NT, preferred_element_type=F32)
                    weights.append(weigh(scores).astype(BF16))
                values = kv_ref[offset : offset + HALF, DH:]
                total_ref[rows, :] += jnp.dot(
                    jnp.concatenate(weights, axis=1), values, preferred_element_type=F32
                )

            @pl.when(reached & jnp.logical_not(whole))
            def _():
                q = q_ref[rows, :]
                begin = jnp.maximum(low - k_first, 0) // TK
                stop = jnp.minimum((q_last - k_first) // TK + 1, HALF // TK)
                q_start = starts_ref[rows, :]
                q_pos = q_first + lax.broadcasted_iota(jnp.int32, (TQ, DH), 0)

                def step(piece, carry):
                    at = pl.multiple_of(offset + piece * TK, TK)
                    keys = kv_ref[pl.ds(at, TK), :DH]
                    values = kv_ref[pl.ds(at, TK), DH:]
                    scores = lax.dot_general(q, keys, NT, preferred_element_type=F32)
                    lanes = lax.broadcasted_iota(jnp.int32, (TQ, DH), 1) + (k_first + piece * TK)
                    allowed = []
                    for strip in range(TK // DH):
                        k_pos = lanes + strip * DH
                        keep = (k_pos >= q_start) & (k_pos <= q_pos)
                        allowed.append(
                            jnp.where(keep, weigh(scores[:, strip * DH : (strip + 1) * DH]), 0.0)
                        )
                    weights = jnp.concatenate(allowed, axis=1).astype(BF16)
                    total_ref[rows, :] += jnp.dot(weights, values, preferred_element_type=F32)
                    return carry

                lax.fori_loop(begin, stop, step, 0)

        return nothing

    lax.fori_loop(0, 2 * ROWS // TQ, one_part, 0)
    if last:
        outs[0][...] = total_ref[:ROWS, :]
        outs[1][...] = total_ref[ROWS:, :]
    else:
        outs[0][...] = total_ref[...]


def attend(place, lengths, q_own, q_sib, blocks, carried=None, last=False):
    count = len(blocks)
    first = carried is None
    pieces = [
        (index, offset, back, corners, shift)
        for index, (block, back, corners, shift) in enumerate(blocks)
        for offset in range(0, block.shape[0], HALF)
    ]
    if first:
        outs = [pltpu.VMEM((2 * ROWS, DH), F32), pltpu.VMEM((2 * ROWS, DH), jnp.int32)]
    elif last:
        outs = [pltpu.VMEM((ROWS, DH), F32)] * 2
    else:
        outs = [pltpu.VMEM((2 * ROWS, DH), F32)]
    arrays = [q_own, q_sib] + [block[0] for block in blocks] + list(() if first else carried)
    return pl.pallas_call(
        functools.partial(attend_kernel, lengths.shape[0], pieces, count, first, last),
        in_specs=[SMEM, SMEM] + [VMEM] * len(arrays),
        out_specs=[VMEM] * len(outs),
        out_shape=outs,
        scratch_shapes=[pltpu.VMEM((2 * ROWS, DH), BF16), pltpu.VMEM((2 * ROWS, DH), F32)],
        compiler_params=pltpu.CompilerParams(vmem_limit_bytes=20 << 20),
        cost_estimate=pl.CostEstimate(
            flops=len(pieces) * 4 * ROWS * ROWS * DH,
            bytes_accessed=4 << 20,
            transcendentals=len(pieces) * ROWS * ROWS,
        ),
        name="attend",
    )(place, lengths, *kept(*arrays))


def gate_kernel(own_ref, sib_ref, u_ref, gain_ref, out_ref):
    attended = own_ref[...] + sib_ref[...]
    centre = jnp.mean(attended, axis=-1, keepdims=True)
    centred = attended - centre
    deviation = jnp.mean(centred * centred, axis=-1, keepdims=True)
    gated = centred * lax.rsqrt(deviation + 1e-05) * gain_ref[...] * u_ref[...].astype(F32)
    out_ref[...] = gated.astype(BF16)


def gate(own, sib, u, gain):
    return pl.pallas_call(
        gate_kernel,
        in_specs=[VMEM] * 4,
        out_specs=VMEM,
        out_shape=pltpu.VMEM(u.shape, BF16),
        compiler_params=pltpu.CompilerParams(vmem_limit_bytes=8 << 20),
        name="gate",
    )(*kept(own, sib, u), gain)


def combine_kernel(heads, parts, place_ref, gated_ref, w_hbm, events_hbm, out_ref, events, w, sems):
    share = events.shape[0]
    deep = w.shape[0] // parts
    fetches = [
        pltpu.make_async_copy(
            w_hbm.at[pl.ds(part * deep, deep)], w.at[pl.ds(part * deep, deep)], sems.at[part]
        )
        for part in range(parts)
    ]
    first = pl.multiple_of(place_ref[1] * share, share)
    fetches.append(pltpu.make_async_copy(events_hbm.at[pl.ds(first, share)], events, sems.at[parts]))
    for fetch in fetches:
        fetch.start()
    gated = jnp.concatenate([gated_ref[head] for head in range(heads)], axis=1)
    total = jnp.zeros((share, w.shape[1]), F32)
    for part in range(parts):
        fetches[part].wait()
        at = slice(part * deep, (part + 1) * deep)
        total += jnp.dot(gated[:, at], w[at, :], preferred_element_type=F32)
    fetches[parts].wait()
    total = (total + events[...].astype(F32)).astype(BF16)
    for head in range(heads):
        out_ref[head] = total[:, head * DH : (head + 1) * DH]


def combine(place, gated, w, events):
    heads, share = gated.shape[:2]
    parts = 4
    hbm = pl.BlockSpec(memory_space=pltpu.HBM)
    return pl.pallas_call(
        functools.partial(combine_kernel, heads, parts),
        in_specs=[SMEM, VMEM, hbm, hbm],
        out_specs=VMEM,
        out_shape=pltpu.VMEM(gated.shape, BF16),
        scratch_shapes=[
            pltpu.VMEM((share, events.shape[1]), BF16),
            pltpu.VMEM(w.shape, BF16),
            pltpu.SemaphoreType.DMA((parts + 1,)),
        ],
        compiler_params=pltpu.CompilerParams(vmem_limit_bytes=8 << 20),
        name="combine",
    )(
        place,
        *kept(gated),
        pltpu.with_memory_space_constraint(w, pltpu.HBM),
        pltpu.with_memory_space_constraint(events, pltpu.HBM),
    )


def on_device(events, lengths, in_gain, w_uvqk, out_gain, w_out):
    rows = events.shape[0]
    heads = lax.axis_size("narrow")
    count = lax.axis_size("wide")
    place = jnp.stack([lax.axis_index("wide"), lax.axis_index("narrow")]).astype(jnp.int32)
    every = (0, 1, 2, 3)

    def moved(value, steps, corners=every):
        pairs = [
            (i, i + steps) for i in range(count) if i // 2 % 4 in corners and 0 <= i + steps < count
        ]
        return lax.ppermute(value, "wide", pairs)

    def swapped(value):
        return lax.ppermute(value, "wide", [(i, i ^ 1) for i in range(count)])

    w_all = lax.all_gather(w_out[0], "narrow", axis=0, tiled=True)
    kv, kva, kvb, q, u = project(events, in_gain, w_uvqk[:, 0, :])
    q_sib = swapped(q)
    back1 = moved(kv, 2, (0, 1, 2))
    back4a = moved(kva, 8)
    back4b = moved(kvb, 8)
    back3w = moved(kv, 6, (0,))
    acc, starts = attend(place, lengths, q, q_sib, [(kv, 0, every, 0)])
    back1, back4a, back4b, acc = lax.optimization_barrier((back1, back4a, back4b, acc))
    back1za = moved(back4a, -6, (3,))
    back3a = moved(back4a, -2, (1, 2, 3))
    back1zb = moved(back4b, -6, (3,))
    back3b = moved(back4b, -2, (1, 2, 3))
    back2 = moved(back1, 2, (1, 2, 3))
    back2a = moved(back1za, 2, (0,))
    back2b = moved(back1zb, 2, (0,))
    nearer = [(back1, 2, (1, 2, 3), 0), (back4a, 8, every, 0), (back4b, 8, every, HALF)]
    acc = attend(place, lengths, q, q_sib, nearer, (starts, acc))[0]
    others = [
        (back1za, 2, (0,), 0),
        (back1zb, 2, (0,), HALF),
        (back3a, 6, (0, 1, 2), 0),
        (back3b, 6, (0, 1, 2), HALF),
        (back3w, 6, (3,), 0),
        (back2, 4, (0, 2, 3), 0),
        (back2a, 4, (1,), 0),
        (back2b, 4, (1,), HALF),
    ]
    own, sib = attend(place, lengths, q, q_sib, others, (starts, acc), True)
    gated = gate(own, swapped(sib), u, out_gain)
    w_all, gated = lax.optimization_barrier((w_all, gated))
    gated = lax.all_to_all(gated.reshape(heads, rows // heads, DH), "narrow", 0, 0)
    out = combine(place, gated, w_all, events)
    return lax.all_to_all(out, "narrow", 0, 0).reshape(rows, DH)


def solution(mesh):
    in_specs = (
        P("wide", None),
        P(),
        P(),
        P(None, "narrow", None),
        P("narrow", None),
        P("narrow", None, None),
    )
    out_specs = P("wide", "narrow")
    return jax.shard_map(
        on_device, mesh=mesh, in_specs=in_specs, out_specs=out_specs, check_vma=False
    )
```

```python
import functools

import jax
import jax.numpy as jnp
from jax import lax
from jax.experimental import pallas as pl
from jax.experimental.pallas import tpu as pltpu
from jax.sharding import PartitionSpec as P

F32 = jnp.float32
BF16 = jnp.bfloat16
SMEM = pl.BlockSpec(memory_space=pltpu.SMEM)
VMEM = pl.BlockSpec(memory_space=pltpu.VMEM)
ROWS = 1024
DH = 128
HALF = 512
TQ = 512
TK = 256
NT = (((1,), (1,)), ((), ()))


def silu(x):
    half = 0.5 * x
    return half + half * jnp.tanh(half)


def kept(*values):
    return [pltpu.with_memory_space_constraint(value, pltpu.VMEM) for value in values]


def project_kernel(
    parts, copies, place_ref, events_hbm, gain_ref, w_hbm, out_hbm,
    kv_ref, q_ref, u_ref, spread_ref, events, w, sems,
):
    rows = events.shape[0] // parts
    half = spread_ref.shape[2]
    columns = pl.ds(pl.multiple_of(place_ref[0] % 2 * half, half), half)
    spreads = [
        pltpu.make_async_copy(out_hbm.at[0, :, columns], spread_ref.at[copy], sems.at[parts + 1 + copy])
        for copy in range(copies)
    ]
    fetch_w = pltpu.make_async_copy(w_hbm, w, sems.at[parts])
    fetches = [
        pltpu.make_async_copy(
            events_hbm.at[pl.ds(part * rows, rows)], events.at[pl.ds(part * rows, rows)], sems.at[part]
        )
        for part in range(parts)
    ]
    fetches[0].start()
    fetch_w.start()
    for fetch in fetches[1:]:
        fetch.start()
    for spread in spreads:
        spread.start()
    for part in range(parts):
        fetches[part].wait()
        x = events[part * rows : (part + 1) * rows, :].astype(F32)
        average = jnp.mean(x, axis=-1, keepdims=True)
        centred = x - average
        variance = jnp.mean(centred * centred, axis=-1, keepdims=True)
        normed = (centred * lax.rsqrt(variance + 1e-05) * gain_ref[...]).astype(BF16)
        if part == 0:
            fetch_w.wait()
        out = silu(jnp.dot(normed, w[...], preferred_element_type=F32)).astype(BF16)
        at = slice(part * rows, (part + 1) * rows)
        u_ref[at, :] = out[:, :DH]
        q_ref[at, :] = out[:, 2 * DH : 3 * DH]
        keys, values = out[:, 3 * DH :], out[:, DH : 2 * DH]
        kv_ref[at, :DH] = keys
        kv_ref[at, DH:] = values
    for spread in spreads:
        spread.wait()


def project(place, events, in_gain, w, w_out, copies):
    rows, width = events.shape
    parts = 4
    hbm = pl.BlockSpec(memory_space=pltpu.HBM)
    return pl.pallas_call(
        functools.partial(project_kernel, parts, copies),
        in_specs=[SMEM, hbm, VMEM, hbm, hbm],
        out_specs=[VMEM] * 4,
        out_shape=[
            pltpu.VMEM((rows, 2 * DH), BF16),
            pltpu.VMEM((rows, DH), BF16),
            pltpu.VMEM((rows, DH), BF16),
            pltpu.VMEM((copies, DH, width // 2), BF16),
        ],
        scratch_shapes=[
            pltpu.VMEM((rows, width), BF16),
            pltpu.VMEM((width, 4 * DH), BF16),
            pltpu.SemaphoreType.DMA((parts + 1 + copies,)),
        ],
        cost_estimate=pl.CostEstimate(
            flops=2 * rows * width * 4 * DH, bytes_accessed=4 << 20, transcendentals=rows * 4 * DH
        ),
        compiler_params=pltpu.CompilerParams(vmem_limit_bytes=20 << 20),
        name="project",
    )(
        place,
        pltpu.with_memory_space_constraint(events, pltpu.HBM),
        in_gain[None],
        pltpu.with_memory_space_constraint(w, pltpu.HBM),
        pltpu.with_memory_space_constraint(w_out, pltpu.HBM),
    )


def attend_kernel(users, pieces, count, first, last, place_ref, lengths_ref, q_own, q_sib, *refs):
    blocks, refs = refs[:count], refs[count:]
    if first:
        outs, starts_ref, q_ref, total_ref = refs[:1], *refs[1:]
    else:
        starts_ref, carried = refs[:2]
        outs, (q_ref, total_ref) = refs[2:-2], refs[-2:]
    me = place_ref[0]
    scale = 0.5 * DH ** (-0.5)

    def weigh(scores):
        half = scores * scale
        return half + half * jnp.tanh(half)

    q_ref[:ROWS, :] = q_own[...]
    q_ref[ROWS:, :] = q_sib[...]
    if first:
        total_ref[...] = jnp.zeros_like(total_ref)
    else:
        total_ref[...] = carried[...]

    def one_part(part, nothing):
        side, inner = part // (ROWS // TQ), part % (ROWS // TQ)
        q_first = jnp.where(side == 0, me, me + 1 - 2 * (me % 2)) * ROWS + inner * TQ
        q_last = q_first + TQ - 1
        rows = pl.ds(pl.multiple_of(part * TQ, TQ), TQ)
        end = jnp.int32(0)
        low = jnp.int32(0)
        high = jnp.int32(0)
        for user in range(users):
            end = end + lengths_ref[user]
            low = jnp.where(end <= q_first, end, low)
            high = jnp.where(end <= q_last, end, high)
        if first:
            starts_ref[rows, :] = jnp.full((TQ, DH), low, jnp.int32)
            end = jnp.int32(0)
            for user in range(users):
                end = end + lengths_ref[user]

                @pl.when((end > q_first) & (end <= q_last))
                def _(end=end):
                    after = q_first + lax.broadcasted_iota(jnp.int32, (TQ, DH), 0) >= end
                    starts_ref[rows, :] = jnp.where(after, end, starts_ref[rows, :])

        for block, offset, back in pieces:
            kv_ref = blocks[block]
            k_first = (me - back) * ROWS + offset
            reached = (me >= back) & (k_first + HALF > low) & (k_first <= q_last)
            whole = (k_first >= high) & (k_first + HALF - 1 <= q_first)

            @pl.when(reached & whole)
            def _():
                q = q_ref[rows, :]
                weights = []
                for piece in range(HALF // TK):
                    keys = kv_ref[offset + piece * TK : offset + (piece + 1) * TK, :DH]
                    scores = lax.dot_general(q, keys, NT, preferred_element_type=F32)
                    weights.append(weigh(scores).astype(BF16))
                values = kv_ref[offset : offset + HALF, DH:]
                total_ref[rows, :] += jnp.dot(
                    jnp.concatenate(weights, axis=1), values, preferred_element_type=F32
                )

            @pl.when(reached & jnp.logical_not(whole))
            def _():
                q = q_ref[rows, :]
                begin = jnp.maximum(low - k_first, 0) // TK
                stop = jnp.minimum((q_last - k_first) // TK + 1, HALF // TK)
                q_start = starts_ref[rows, :]
                q_pos = q_first + lax.broadcasted_iota(jnp.int32, (TQ, DH), 0)

                def step(piece, carry):
                    at = pl.multiple_of(offset + piece * TK, TK)
                    keys = kv_ref[pl.ds(at, TK), :DH]
                    values = kv_ref[pl.ds(at, TK), DH:]
                    scores = lax.dot_general(q, keys, NT, preferred_element_type=F32)
                    lanes = lax.broadcasted_iota(jnp.int32, (TQ, DH), 1) + (k_first + piece * TK)
                    allowed = []
                    for strip in range(TK // DH):
                        k_pos = lanes + strip * DH
                        keep = (k_pos >= q_start) & (k_pos <= q_pos)
                        allowed.append(
                            jnp.where(keep, weigh(scores[:, strip * DH : (strip + 1) * DH]), 0.0)
                        )
                    weights = jnp.concatenate(allowed, axis=1).astype(BF16)
                    total_ref[rows, :] += jnp.dot(weights, values, preferred_element_type=F32)
                    return carry

                lax.fori_loop(begin, stop, step, 0)

        return nothing

    lax.fori_loop(0, 2 * ROWS // TQ, one_part, 0)
    if last:
        outs[0][...] = total_ref[:ROWS, :]
        outs[1][...] = total_ref[ROWS:, :]
    else:
        outs[0][...] = total_ref[...]


def attend(place, lengths, q_own, q_sib, blocks, carried=None, weight=1, last=False):
    count = len(blocks)
    first = carried is None
    pieces = [
        (index, offset, back)
        for index, (block, back) in enumerate(blocks)
        for offset in range(0, block.shape[0], HALF)
    ]
    if first:
        outs = [pltpu.VMEM((2 * ROWS, DH), F32), pltpu.VMEM((2 * ROWS, DH), jnp.int32)]
    elif last:
        outs = [pltpu.VMEM((ROWS, DH), F32)] * 2
    else:
        outs = [pltpu.VMEM((2 * ROWS, DH), F32)]
    arrays = [q_own, q_sib] + [block[0] for block in blocks] + list(() if first else carried)
    return pl.pallas_call(
        functools.partial(attend_kernel, lengths.shape[0], pieces, count, first, last),
        in_specs=[SMEM, SMEM] + [VMEM] * len(arrays),
        out_specs=[VMEM] * len(outs),
        out_shape=outs,
        scratch_shapes=[pltpu.VMEM((2 * ROWS, DH), BF16), pltpu.VMEM((2 * ROWS, DH), F32)],
        compiler_params=pltpu.CompilerParams(vmem_limit_bytes=20 << 20),
        cost_estimate=pl.CostEstimate(
            flops=weight * len(pieces) * 4 * ROWS * ROWS * DH,
            bytes_accessed=weight << 20,
            transcendentals=weight * len(pieces) * ROWS * ROWS,
        ),
        name="attend",
    )(place, lengths, *kept(*arrays))


def gate_kernel(own_ref, sib_ref, u_ref, gain_ref, out_ref):
    attended = own_ref[...] + sib_ref[...]
    centre = jnp.mean(attended, axis=-1, keepdims=True)
    centred = attended - centre
    deviation = jnp.mean(centred * centred, axis=-1, keepdims=True)
    gated = centred * lax.rsqrt(deviation + 1e-05) * gain_ref[...] * u_ref[...].astype(F32)
    out_ref[...] = gated.astype(BF16)


def gate(own, sib, u, gain):
    return pl.pallas_call(
        gate_kernel,
        in_specs=[VMEM] * 4,
        out_specs=VMEM,
        out_shape=pltpu.VMEM(u.shape, BF16),
        compiler_params=pltpu.CompilerParams(vmem_limit_bytes=8 << 20),
        name="gate",
    )(*kept(own, sib, u), gain)


def combine_kernel(heads, place_ref, gated_ref, mine_ref, other_ref, events_hbm, out_ref, events, sem):
    share = events.shape[0]
    fetch = pltpu.make_async_copy(
        events_hbm.at[pl.ds(pl.multiple_of(place_ref[1] * share, share), share)], events, sem
    )
    fetch.start()
    gated = jnp.concatenate([gated_ref[head] for head in range(heads)], axis=1)
    half = heads // 2
    core = place_ref[0] % 2
    totals = [
        jnp.dot(gated, w_ref[...].reshape(heads * DH, half * DH), preferred_element_type=F32)
        for w_ref in (mine_ref, other_ref)
    ]
    fetch.wait()
    for total, side in zip(totals, (core, 1 - core)):
        columns = pl.ds(pl.multiple_of(side * half * DH, half * DH), half * DH)
        total = (total + events[:, columns].astype(F32)).astype(BF16)
        for part in range(half):
            out_ref[side * half + part] = total[:, part * DH : (part + 1) * DH]


def combine(place, gated, mine, other, events):
    heads, share = gated.shape[:2]
    return pl.pallas_call(
        functools.partial(combine_kernel, heads),
        in_specs=[SMEM] + [VMEM] * 3 + [pl.BlockSpec(memory_space=pltpu.HBM)],
        out_specs=VMEM,
        out_shape=pltpu.VMEM(gated.shape, BF16),
        scratch_shapes=[pltpu.VMEM((share, events.shape[1]), BF16), pltpu.SemaphoreType.DMA],
        compiler_params=pltpu.CompilerParams(vmem_limit_bytes=8 << 20),
        name="combine",
    )(place, *kept(gated, mine, other), pltpu.with_memory_space_constraint(events, pltpu.HBM))


def on_device(events, lengths, in_gain, w_uvqk, out_gain, w_out):
    rows = events.shape[0]
    heads = lax.axis_size("narrow")
    count = lax.axis_size("wide")
    place = jnp.stack([lax.axis_index("wide"), lax.axis_index("narrow")]).astype(jnp.int32)

    def moved(value, steps):
        pairs = [(i, i + steps) for i in range(count) if 0 <= i + steps < count]
        return lax.ppermute(value, "wide", pairs)

    def swapped(value):
        return lax.ppermute(value, "wide", [(i, i ^ 1) for i in range(count)])

    kv, q, u, spread = project(place, events, in_gain, w_uvqk[:, 0, :], w_out, heads)
    q_sib = swapped(q)
    back1 = moved(kv, 2)
    back4 = moved(kv, 8)
    acc, starts = attend(place, lengths, q, q_sib, [(kv, 0)], weight=0)
    spread, acc = lax.optimization_barrier((spread, acc))
    w_half = lax.all_to_all(spread, "narrow", 0, 0)
    back1, back4, acc = lax.optimization_barrier((back1, back4, acc))
    back2 = moved(back1, 2)
    back3 = moved(back4, -2)
    acc = attend(place, lengths, q, q_sib, [(back1, 2), (back4, 8)], (starts, acc), weight=50)[0]
    others = [(back2, 4), (back3, 6)]
    own, sib = attend(place, lengths, q, q_sib, others, (starts, acc), 50, True)
    gated = gate(own, swapped(sib), u, out_gain)
    w_half, gated = lax.optimization_barrier((w_half, gated))
    w_other = swapped(w_half)
    gated = lax.all_to_all(gated.reshape(heads, rows // heads, DH), "narrow", 0, 0)
    out = combine(place, gated, w_half, w_other, events)
    return lax.all_to_all(out, "narrow", 0, 0).reshape(rows, DH)


def solution(mesh):
    in_specs = (
        P("wide", None),
        P(),
        P(),
        P(None, "narrow", None),
        P("narrow", None),
        P("narrow", None, None),
    )
    out_specs = P("wide", "narrow")
    return jax.shard_map(
        on_device, mesh=mesh, in_specs=in_specs, out_specs=out_specs, check_vma=False
    )
```

```python
import functools

import jax
import jax.numpy as jnp
from jax import lax
from jax.experimental import pallas as pl
from jax.experimental.pallas import tpu as pltpu
from jax.sharding import PartitionSpec as P

F32 = jnp.float32
BF16 = jnp.bfloat16
SMEM = pl.BlockSpec(memory_space=pltpu.SMEM)
VMEM = pl.BlockSpec(memory_space=pltpu.VMEM)
ROWS = 1024
DH = 128
HALF = 512
TQ = 512
TK = 256
NT = (((1,), (1,)), ((), ()))


def silu(x):
    half = 0.5 * x
    return half + half * jnp.tanh(half)


def kept(*values):
    return [pltpu.with_memory_space_constraint(value, pltpu.VMEM) for value in values]


def project_kernel(
    parts, events_hbm, gain_hbm, w_hbm, kv_hbm, q_ref, u_hbm, events, gain, w, kv_ref, u_ref, sems, out_sems
):
    rows = events.shape[0] // parts
    fetch_w = pltpu.make_async_copy(w_hbm, w, sems.at[parts])
    fetch_gain = pltpu.make_async_copy(gain_hbm, gain, sems.at[parts + 1])
    fetches = [
        pltpu.make_async_copy(
            events_hbm.at[pl.ds(part * rows, rows)], events.at[pl.ds(part * rows, rows)], sems.at[part]
        )
        for part in range(parts)
    ]
    fetches[0].start()
    fetch_gain.start()
    fetch_w.start()
    for fetch in fetches[1:]:
        fetch.start()
    stores = []
    for part in range(parts):
        fetches[part].wait()
        x = events[part * rows : (part + 1) * rows, :].astype(F32)
        average = jnp.mean(x, axis=-1, keepdims=True)
        centred = x - average
        variance = jnp.mean(centred * centred, axis=-1, keepdims=True)
        if part == 0:
            fetch_gain.wait()
        normed = (centred * lax.rsqrt(variance + 1e-05) * gain[...]).astype(BF16)
        if part == 0:
            fetch_w.wait()
        out = silu(jnp.dot(normed, w[...], preferred_element_type=F32)).astype(BF16)
        at = slice(part * rows, (part + 1) * rows)
        u_ref[at, :] = out[:, :DH]
        q_ref[at, :] = out[:, 2 * DH : 3 * DH]
        keys, values = out[:, 3 * DH :], out[:, DH : 2 * DH]
        kv_ref[at, :DH] = keys
        kv_ref[at, DH:] = values
        at = pl.ds(part * rows, rows)
        for index, (value_ref, value_hbm) in enumerate(((kv_ref, kv_hbm), (u_ref, u_hbm))):
            store = pltpu.make_async_copy(value_ref.at[at], value_hbm.at[at], out_sems.at[part, index])
            store.start()
            stores.append(store)
    for store in stores:
        store.wait()


def project(events, in_gain, w):
    rows, width = events.shape
    parts = 4
    hbm = pl.BlockSpec(memory_space=pltpu.HBM)
    return pl.pallas_call(
        functools.partial(project_kernel, parts),
        in_specs=[hbm] * 3,
        out_specs=[hbm, VMEM, hbm],
        out_shape=[
            pltpu.HBM((rows, 2 * DH), BF16),
            pltpu.VMEM((rows, DH), BF16),
            pltpu.HBM((rows, DH), BF16),
        ],
        scratch_shapes=[
            pltpu.VMEM((rows, width), BF16),
            pltpu.VMEM((1, width), F32),
            pltpu.VMEM((width, 4 * DH), BF16),
            pltpu.VMEM((rows, 2 * DH), BF16),
            pltpu.VMEM((rows, DH), BF16),
            pltpu.SemaphoreType.DMA((parts + 2,)),
            pltpu.SemaphoreType.DMA((parts, 2)),
        ],
        cost_estimate=pl.CostEstimate(
            flops=2 * rows * width * 4 * DH, bytes_accessed=4 << 20, transcendentals=rows * 4 * DH
        ),
        compiler_params=pltpu.CompilerParams(vmem_limit_bytes=20 << 20),
        name="project",
    )(*[pltpu.with_memory_space_constraint(value, pltpu.HBM) for value in (events, in_gain[None], w)])


def attend_kernel(users, pieces, count, first, last, place_ref, lengths_ref, q_own, q_sib, *refs):
    blocks, refs = refs[:count], refs[count:]
    if first:
        out_hbm, total_out, starts_ref, spread_ref, q_ref, total_ref, sems = refs
        outs = [total_out]
        copies, _, half = spread_ref.shape
        columns = pl.ds(pl.multiple_of(place_ref[0] % 2 * half, half), half)
        spreads = [
            pltpu.make_async_copy(out_hbm.at[0, :, columns], spread_ref.at[copy], sems.at[copy])
            for copy in range(copies)
        ]
        for spread in spreads:
            spread.start()
    else:
        starts_ref, carried = refs[:2]
        outs, (q_ref, total_ref) = refs[2:-2], refs[-2:]
    me = place_ref[0]
    scale = 0.5 * DH ** (-0.5)

    def weigh(scores):
        half = scores * scale
        return half + half * jnp.tanh(half)

    q_ref[:ROWS, :] = q_own[...]
    q_ref[ROWS:, :] = q_sib[...]
    if first:
        total_ref[...] = jnp.zeros_like(total_ref)
    else:
        total_ref[...] = carried[...]

    def one_part(part, nothing):
        side, inner = part // (ROWS // TQ), part % (ROWS // TQ)
        q_first = jnp.where(side == 0, me, me + 1 - 2 * (me % 2)) * ROWS + inner * TQ
        q_last = q_first + TQ - 1
        rows = pl.ds(pl.multiple_of(part * TQ, TQ), TQ)
        end = jnp.int32(0)
        low = jnp.int32(0)
        high = jnp.int32(0)
        for user in range(users):
            end = end + lengths_ref[user]
            low = jnp.where(end <= q_first, end, low)
            high = jnp.where(end <= q_last, end, high)
        if first:
            starts_ref[rows, :] = jnp.full((TQ, DH), low, jnp.int32)
            end = jnp.int32(0)
            for user in range(users):
                end = end + lengths_ref[user]

                @pl.when((end > q_first) & (end <= q_last))
                def _(end=end):
                    after = q_first + lax.broadcasted_iota(jnp.int32, (TQ, DH), 0) >= end
                    starts_ref[rows, :] = jnp.where(after, end, starts_ref[rows, :])

        for block, offset, back in pieces:
            kv_ref = blocks[block]
            k_first = (me - back) * ROWS + offset
            reached = (me >= back) & (k_first + HALF > low) & (k_first <= q_last)
            whole = (k_first >= high) & (k_first + HALF - 1 <= q_first)

            @pl.when(reached & whole)
            def _():
                q = q_ref[rows, :]
                weights = []
                for piece in range(HALF // TK):
                    keys = kv_ref[offset + piece * TK : offset + (piece + 1) * TK, :DH]
                    scores = lax.dot_general(q, keys, NT, preferred_element_type=F32)
                    weights.append(weigh(scores).astype(BF16))
                values = kv_ref[offset : offset + HALF, DH:]
                total_ref[rows, :] += jnp.dot(
                    jnp.concatenate(weights, axis=1), values, preferred_element_type=F32
                )

            @pl.when(reached & jnp.logical_not(whole))
            def _():
                q = q_ref[rows, :]
                begin = jnp.maximum(low - k_first, 0) // TK
                stop = jnp.minimum((q_last - k_first) // TK + 1, HALF // TK)
                q_start = starts_ref[rows, :]
                q_pos = q_first + lax.broadcasted_iota(jnp.int32, (TQ, DH), 0)

                def step(piece, carry):
                    at = pl.multiple_of(offset + piece * TK, TK)
                    keys = kv_ref[pl.ds(at, TK), :DH]
                    values = kv_ref[pl.ds(at, TK), DH:]
                    scores = lax.dot_general(q, keys, NT, preferred_element_type=F32)
                    lanes = lax.broadcasted_iota(jnp.int32, (TQ, DH), 1) + (k_first + piece * TK)
                    allowed = []
                    for strip in range(TK // DH):
                        k_pos = lanes + strip * DH
                        keep = (k_pos >= q_start) & (k_pos <= q_pos)
                        allowed.append(
                            jnp.where(keep, weigh(scores[:, strip * DH : (strip + 1) * DH]), 0.0)
                        )
                    weights = jnp.concatenate(allowed, axis=1).astype(BF16)
                    total_ref[rows, :] += jnp.dot(weights, values, preferred_element_type=F32)
                    return carry

                lax.fori_loop(begin, stop, step, 0)

        return nothing

    lax.fori_loop(0, 2 * ROWS // TQ, one_part, 0)
    if first:
        for spread in spreads:
            spread.wait()
    if last:
        outs[0][...] = total_ref[:ROWS, :]
        outs[1][...] = total_ref[ROWS:, :].astype(BF16)
    else:
        outs[0][...] = total_ref[...]


def attend(place, lengths, q_own, q_sib, blocks, carried=None, weight=1, last=False, w_out=None, copies=1):
    count = len(blocks)
    first = carried is None
    pieces = [
        (index, offset, back)
        for index, (block, back) in enumerate(blocks)
        for offset in range(0, block.shape[0], HALF)
    ]
    if first:
        outs = [
            pltpu.VMEM((2 * ROWS, DH), F32),
            pltpu.VMEM((2 * ROWS, DH), jnp.int32),
            pltpu.HBM((copies, DH, w_out.shape[2] // 2), BF16),
        ]
    elif last:
        outs = [pltpu.VMEM((ROWS, DH), F32), pltpu.VMEM((ROWS, DH), BF16)]
    else:
        outs = [pltpu.VMEM((2 * ROWS, DH), F32)]
    arrays = kept(q_own, q_sib, *[block[0] for block in blocks], *(() if first else carried))
    specs = [SMEM, SMEM] + [VMEM] * len(arrays)
    scratch = [pltpu.VMEM((2 * ROWS, DH), BF16), pltpu.VMEM((2 * ROWS, DH), F32)]
    if first:
        arrays.append(pltpu.with_memory_space_constraint(w_out, pltpu.HBM))
        specs.append(pl.BlockSpec(memory_space=pltpu.HBM))
        scratch.append(pltpu.SemaphoreType.DMA((copies,)))
    return pl.pallas_call(
        functools.partial(attend_kernel, lengths.shape[0], pieces, count, first, last),
        in_specs=specs,
        out_specs=[VMEM, VMEM, pl.BlockSpec(memory_space=pltpu.HBM)] if first else [VMEM] * len(outs),
        out_shape=outs,
        scratch_shapes=scratch,
        compiler_params=pltpu.CompilerParams(vmem_limit_bytes=20 << 20),
        cost_estimate=pl.CostEstimate(
            flops=weight * len(pieces) * 4 * ROWS * ROWS * DH,
            bytes_accessed=4 << 20,
            transcendentals=weight * len(pieces) * ROWS * ROWS,
        ),
        name="attend",
    )(place, lengths, *arrays)


def gate_kernel(own_ref, sib_ref, u_ref, gain_ref, out_ref):
    attended = own_ref[...] + sib_ref[...].astype(F32)
    centre = jnp.mean(attended, axis=-1, keepdims=True)
    centred = attended - centre
    deviation = jnp.mean(centred * centred, axis=-1, keepdims=True)
    gated = centred * lax.rsqrt(deviation + 1e-05) * gain_ref[...] * u_ref[...].astype(F32)
    out_ref[...] = gated.astype(BF16)


def gate(own, sib, u, gain):
    return pl.pallas_call(
        gate_kernel,
        in_specs=[VMEM] * 4,
        out_specs=VMEM,
        out_shape=pltpu.VMEM(u.shape, BF16),
        compiler_params=pltpu.CompilerParams(vmem_limit_bytes=8 << 20),
        name="gate",
    )(*kept(own, sib), u, gain)


def combine_kernel(heads, place_ref, gated_ref, mine_ref, other_ref, events_hbm, out_ref, events, sem):
    share = events.shape[0]
    fetch = pltpu.make_async_copy(
        events_hbm.at[pl.ds(pl.multiple_of(place_ref[1] * share, share), share)], events, sem
    )
    fetch.start()
    gated = jnp.concatenate([gated_ref[head] for head in range(heads)], axis=1)
    half = heads // 2
    core = place_ref[0] % 2
    totals = [
        jnp.dot(gated, w_ref[...].reshape(heads * DH, half * DH), preferred_element_type=F32)
        for w_ref in (mine_ref, other_ref)
    ]
    fetch.wait()
    for total, side in zip(totals, (core, 1 - core)):
        columns = pl.ds(pl.multiple_of(side * half * DH, half * DH), half * DH)
        total = (total + events[:, columns].astype(F32)).astype(BF16)
        for part in range(half):
            out_ref[side * half + part] = total[:, part * DH : (part + 1) * DH]


def combine(place, gated, mine, other, events):
    heads, share = gated.shape[:2]
    return pl.pallas_call(
        functools.partial(combine_kernel, heads),
        in_specs=[SMEM] + [VMEM] * 3 + [pl.BlockSpec(memory_space=pltpu.HBM)],
        out_specs=VMEM,
        out_shape=pltpu.VMEM(gated.shape, BF16),
        scratch_shapes=[pltpu.VMEM((share, events.shape[1]), BF16), pltpu.SemaphoreType.DMA],
        compiler_params=pltpu.CompilerParams(vmem_limit_bytes=8 << 20),
        name="combine",
    )(place, *kept(gated, mine, other), pltpu.with_memory_space_constraint(events, pltpu.HBM))


def on_device(events, lengths, in_gain, w_uvqk, out_gain, w_out):
    rows = events.shape[0]
    heads = lax.axis_size("narrow")
    count = lax.axis_size("wide")
    place = jnp.stack([lax.axis_index("wide"), lax.axis_index("narrow")]).astype(jnp.int32)

    def moved(value, steps):
        pairs = [(i, (i + steps) % count) for i in range(count)]
        return lax.ppermute(value, "wide", pairs)

    def swapped(value):
        return lax.ppermute(value, "wide", [(i, i ^ 1) for i in range(count)])

    kv, q, u = project(events, in_gain, w_uvqk[:, 0, :])
    q_sib = swapped(q)
    back1 = moved(kv, 2)
    back4 = moved(kv, 8)
    acc, starts, spread = attend(
        place, lengths, q, q_sib, [(kv, 0)], weight=0, w_out=w_out, copies=heads
    )
    spread, acc = lax.optimization_barrier((spread, acc))
    w_half = lax.all_to_all(spread, "narrow", 0, 0)
    back1, acc = lax.optimization_barrier((back1, acc))
    back2 = moved(back1, 2)
    back3 = moved(back4, -2)
    acc = attend(place, lengths, q, q_sib, [(back1, 2), (back4, 8)], (starts, acc), weight=0)[0]
    acc = attend(place, lengths, q, q_sib, [(back2, 4)], (starts, acc), weight=50)[0]
    own, sib = attend(place, lengths, q, q_sib, [(back3, 6)], (starts, acc), weight=50, last=True)
    gated = gate(own, swapped(sib), u, out_gain)
    w_half, gated = lax.optimization_barrier((w_half, gated))
    w_other = swapped(w_half)
    gated = lax.all_to_all(gated.reshape(heads, rows // heads, DH), "narrow", 0, 0)
    out = combine(place, gated, w_half, w_other, events)
    return lax.all_to_all(out, "narrow", 0, 0).reshape(rows, DH)


def solution(mesh):
    in_specs = (
        P("wide", None),
        P(),
        P(),
        P(None, "narrow", None),
        P("narrow", None),
        P("narrow", None, None),
    )
    out_specs = P("wide", "narrow")
    return jax.shard_map(
        on_device, mesh=mesh, in_specs=in_specs, out_specs=out_specs, check_vma=False
    )
```

```python
import functools

import jax
import jax.numpy as jnp
from jax import lax
from jax.experimental import pallas as pl
from jax.experimental.pallas import tpu as pltpu
from jax.sharding import PartitionSpec as P

F32 = jnp.float32
BF16 = jnp.bfloat16
SMEM = pl.BlockSpec(memory_space=pltpu.SMEM)
VMEM = pl.BlockSpec(memory_space=pltpu.VMEM)
ROWS = 1024
DH = 128
HALF = 512
TQ = 512
TK = 256
NT = (((1,), (1,)), ((), ()))


def silu(x):
    half = 0.5 * x
    return half + half * jnp.tanh(half)


def kept(*values):
    return [pltpu.with_memory_space_constraint(value, pltpu.VMEM) for value in values]


def project_kernel(
    parts, place_ref, events_hbm, gain_hbm, w_hbm, w_out_hbm, kv_hbm, q_ref, u_hbm, spread_hbm,
    events, gain, w, w_half, kv_ref, u_ref, sems, out_sems, spread_sems,
):
    rows = events.shape[0] // parts
    fetch_w = pltpu.make_async_copy(w_hbm, w, sems.at[parts])
    fetch_gain = pltpu.make_async_copy(gain_hbm, gain, sems.at[parts + 1])
    fetches = [
        pltpu.make_async_copy(
            events_hbm.at[pl.ds(part * rows, rows)], events.at[pl.ds(part * rows, rows)], sems.at[part]
        )
        for part in range(parts)
    ]
    half = w_half.shape[1]
    columns = pl.ds(pl.multiple_of(place_ref[0] % 2 * half, half), half)
    fetch_half = pltpu.make_async_copy(w_out_hbm.at[0, :, columns], w_half, sems.at[parts + 2])
    fetches[0].start()
    fetch_gain.start()
    fetch_w.start()
    for fetch in fetches[1:]:
        fetch.start()
    fetch_half.start()
    stores = []
    for part in range(parts):
        fetches[part].wait()
        x = events[part * rows : (part + 1) * rows, :].astype(F32)
        average = jnp.mean(x, axis=-1, keepdims=True)
        centred = x - average
        variance = jnp.mean(centred * centred, axis=-1, keepdims=True)
        if part == 0:
            fetch_gain.wait()
        normed = (centred * lax.rsqrt(variance + 1e-05) * gain[...]).astype(BF16)
        if part == 0:
            fetch_w.wait()
        out = silu(jnp.dot(normed, w[...], preferred_element_type=F32)).astype(BF16)
        at = slice(part * rows, (part + 1) * rows)
        u_ref[at, :] = out[:, :DH]
        q_ref[at, :] = out[:, 2 * DH : 3 * DH]
        keys, values = out[:, 3 * DH :], out[:, DH : 2 * DH]
        kv_ref[at, :DH] = keys
        kv_ref[at, DH:] = values
        at = pl.ds(part * rows, rows)
        for index, (value_ref, value_hbm) in enumerate(((kv_ref, kv_hbm), (u_ref, u_hbm))):
            store = pltpu.make_async_copy(value_ref.at[at], value_hbm.at[at], out_sems.at[part, index])
            store.start()
            stores.append(store)
        if part == 0:
            fetch_half.wait()
            for copy in range(spread_hbm.shape[0]):
                store = pltpu.make_async_copy(w_half, spread_hbm.at[copy], spread_sems.at[copy])
                store.start()
                stores.append(store)
    for store in stores:
        store.wait()


def project(place, events, in_gain, w, w_out, copies):
    rows, width = events.shape
    parts = 4
    hbm = pl.BlockSpec(memory_space=pltpu.HBM)
    return pl.pallas_call(
        functools.partial(project_kernel, parts),
        in_specs=[SMEM] + [hbm] * 4,
        out_specs=[hbm, VMEM, hbm, hbm],
        out_shape=[
            pltpu.HBM((rows, 2 * DH), BF16),
            pltpu.VMEM((rows, DH), BF16),
            pltpu.HBM((rows, DH), BF16),
            pltpu.HBM((copies, DH, width // 2), BF16),
        ],
        scratch_shapes=[
            pltpu.VMEM((rows, width), BF16),
            pltpu.VMEM((1, width), F32),
            pltpu.VMEM((width, 4 * DH), BF16),
            pltpu.VMEM((DH, width // 2), BF16),
            pltpu.VMEM((rows, 2 * DH), BF16),
            pltpu.VMEM((rows, DH), BF16),
            pltpu.SemaphoreType.DMA((parts + 3,)),
            pltpu.SemaphoreType.DMA((parts, 2)),
            pltpu.SemaphoreType.DMA((copies,)),
        ],
        cost_estimate=pl.CostEstimate(
            flops=2 * rows * width * 4 * DH, bytes_accessed=4 << 20, transcendentals=rows * 4 * DH
        ),
        compiler_params=pltpu.CompilerParams(vmem_limit_bytes=20 << 20),
        name="project",
    )(
        place,
        *[pltpu.with_memory_space_constraint(value, pltpu.HBM) for value in (events, in_gain[None], w, w_out)],
    )


def attend_kernel(users, pieces, count, first, last, place_ref, lengths_ref, q_own, q_sib, *refs):
    blocks, refs = refs[:count], refs[count:]
    if first:
        total_out, starts_ref, q_ref, total_ref = refs
        outs = [total_out]
    else:
        starts_ref, carried = refs[:2]
        outs, (q_ref, total_ref) = refs[2:-2], refs[-2:]
    me = place_ref[0]
    scale = 0.5 * DH ** (-0.5)

    def weigh(scores):
        half = scores * scale
        return half + half * jnp.tanh(half)

    q_ref[:ROWS, :] = q_own[...]
    q_ref[ROWS:, :] = q_sib[...]
    if first:
        total_ref[...] = jnp.zeros_like(total_ref)
    else:
        total_ref[...] = carried[...]

    def one_part(part, nothing):
        side, inner = part // (ROWS // TQ), part % (ROWS // TQ)
        q_first = jnp.where(side == 0, me, me + 1 - 2 * (me % 2)) * ROWS + inner * TQ
        q_last = q_first + TQ - 1
        rows = pl.ds(pl.multiple_of(part * TQ, TQ), TQ)
        end = jnp.int32(0)
        low = jnp.int32(0)
        high = jnp.int32(0)
        for user in range(users):
            end = end + lengths_ref[user]
            low = jnp.where(end <= q_first, end, low)
            high = jnp.where(end <= q_last, end, high)
        if first:
            starts_ref[rows, :] = jnp.full((TQ, DH), low, jnp.int32)
            end = jnp.int32(0)
            for user in range(users):
                end = end + lengths_ref[user]

                @pl.when((end > q_first) & (end <= q_last))
                def _(end=end):
                    after = q_first + lax.broadcasted_iota(jnp.int32, (TQ, DH), 0) >= end
                    starts_ref[rows, :] = jnp.where(after, end, starts_ref[rows, :])

        for block, offset, back in pieces:
            kv_ref = blocks[block]
            k_first = (me - back) * ROWS + offset
            reached = (me >= back) & (k_first + HALF > low) & (k_first <= q_last)
            whole = (k_first >= high) & (k_first + HALF - 1 <= q_first)

            @pl.when(reached & whole)
            def _():
                q = q_ref[rows, :]
                weights = []
                for piece in range(HALF // TK):
                    keys = kv_ref[offset + piece * TK : offset + (piece + 1) * TK, :DH]
                    scores = lax.dot_general(q, keys, NT, preferred_element_type=F32)
                    weights.append(weigh(scores).astype(BF16))
                values = kv_ref[offset : offset + HALF, DH:]
                total_ref[rows, :] += jnp.dot(
                    jnp.concatenate(weights, axis=1), values, preferred_element_type=F32
                )

            @pl.when(reached & jnp.logical_not(whole))
            def _():
                q = q_ref[rows, :]
                begin = jnp.maximum(low - k_first, 0) // TK
                stop = jnp.minimum((q_last - k_first) // TK + 1, HALF // TK)
                q_start = starts_ref[rows, :]
                q_pos = q_first + lax.broadcasted_iota(jnp.int32, (TQ, DH), 0)

                def step(piece, carry):
                    at = pl.multiple_of(offset + piece * TK, TK)
                    keys = kv_ref[pl.ds(at, TK), :DH]
                    values = kv_ref[pl.ds(at, TK), DH:]
                    scores = lax.dot_general(q, keys, NT, preferred_element_type=F32)
                    lanes = lax.broadcasted_iota(jnp.int32, (TQ, DH), 1) + (k_first + piece * TK)
                    allowed = []
                    for strip in range(TK // DH):
                        k_pos = lanes + strip * DH
                        keep = (k_pos >= q_start) & (k_pos <= q_pos)
                        allowed.append(
                            jnp.where(keep, weigh(scores[:, strip * DH : (strip + 1) * DH]), 0.0)
                        )
                    weights = jnp.concatenate(allowed, axis=1).astype(BF16)
                    total_ref[rows, :] += jnp.dot(weights, values, preferred_element_type=F32)
                    return carry

                lax.fori_loop(begin, stop, step, 0)

        return nothing

    lax.fori_loop(0, 2 * ROWS // TQ, one_part, 0)
    if last:
        outs[0][...] = total_ref[:ROWS, :]
        outs[1][...] = total_ref[ROWS:, :].astype(BF16)
    else:
        outs[0][...] = total_ref[...]


def attend(place, lengths, q_own, q_sib, blocks, carried=None, weight=1, last=False):
    count = len(blocks)
    first = carried is None
    pieces = [
        (index, offset, back)
        for index, (block, back) in enumerate(blocks)
        for offset in range(0, block.shape[0], HALF)
    ]
    if first:
        outs = [
            pltpu.VMEM((2 * ROWS, DH), F32),
            pltpu.VMEM((2 * ROWS, DH), jnp.int32),
        ]
    elif last:
        outs = [pltpu.VMEM((ROWS, DH), F32), pltpu.VMEM((ROWS, DH), BF16)]
    else:
        outs = [pltpu.VMEM((2 * ROWS, DH), F32)]
    arrays = kept(q_own, q_sib, *[block[0] for block in blocks], *(() if first else carried))
    specs = [SMEM, SMEM] + [VMEM] * len(arrays)
    scratch = [pltpu.VMEM((2 * ROWS, DH), BF16), pltpu.VMEM((2 * ROWS, DH), F32)]
    return pl.pallas_call(
        functools.partial(attend_kernel, lengths.shape[0], pieces, count, first, last),
        in_specs=specs,
        out_specs=[VMEM] * len(outs),
        out_shape=outs,
        scratch_shapes=scratch,
        compiler_params=pltpu.CompilerParams(vmem_limit_bytes=20 << 20),
        cost_estimate=pl.CostEstimate(
            flops=weight * len(pieces) * 4 * ROWS * ROWS * DH,
            bytes_accessed=4 << 20,
            transcendentals=weight * len(pieces) * ROWS * ROWS,
        ),
        name="attend",
    )(place, lengths, *arrays)


def gate_kernel(own_ref, sib_ref, u_ref, gain_ref, out_ref):
    attended = own_ref[...] + sib_ref[...].astype(F32)
    centre = jnp.mean(attended, axis=-1, keepdims=True)
    centred = attended - centre
    deviation = jnp.mean(centred * centred, axis=-1, keepdims=True)
    gated = centred * lax.rsqrt(deviation + 1e-05) * gain_ref[...] * u_ref[...].astype(F32)
    out_ref[...] = gated.astype(BF16)


def gate(own, sib, u, gain):
    return pl.pallas_call(
        gate_kernel,
        in_specs=[VMEM] * 4,
        out_specs=VMEM,
        out_shape=pltpu.VMEM(u.shape, BF16),
        compiler_params=pltpu.CompilerParams(vmem_limit_bytes=8 << 20),
        name="gate",
    )(*kept(own, sib), u, gain)


def combine_kernel(heads, place_ref, gated_ref, mine_ref, other_ref, events_hbm, out_ref, events, sem):
    share = events.shape[0]
    fetch = pltpu.make_async_copy(
        events_hbm.at[pl.ds(pl.multiple_of(place_ref[1] * share, share), share)], events, sem
    )
    fetch.start()
    gated = jnp.concatenate([gated_ref[head] for head in range(heads)], axis=1)
    half = heads // 2
    core = place_ref[0] % 2
    totals = [
        jnp.dot(gated, w_ref[...].reshape(heads * DH, half * DH), preferred_element_type=F32)
        for w_ref in (mine_ref, other_ref)
    ]
    fetch.wait()
    for total, side in zip(totals, (core, 1 - core)):
        columns = pl.ds(pl.multiple_of(side * half * DH, half * DH), half * DH)
        total = (total + events[:, columns].astype(F32)).astype(BF16)
        for part in range(half):
            out_ref[side * half + part] = total[:, part * DH : (part + 1) * DH]


def combine(place, gated, mine, other, events):
    heads, share = gated.shape[:2]
    return pl.pallas_call(
        functools.partial(combine_kernel, heads),
        in_specs=[SMEM] + [VMEM] * 3 + [pl.BlockSpec(memory_space=pltpu.HBM)],
        out_specs=VMEM,
        out_shape=pltpu.VMEM(gated.shape, BF16),
        scratch_shapes=[pltpu.VMEM((share, events.shape[1]), BF16), pltpu.SemaphoreType.DMA],
        compiler_params=pltpu.CompilerParams(vmem_limit_bytes=8 << 20),
        name="combine",
    )(place, *kept(gated, mine, other), pltpu.with_memory_space_constraint(events, pltpu.HBM))


def on_device(events, lengths, in_gain, w_uvqk, out_gain, w_out):
    rows = events.shape[0]
    heads = lax.axis_size("narrow")
    count = lax.axis_size("wide")
    place = jnp.stack([lax.axis_index("wide"), lax.axis_index("narrow")]).astype(jnp.int32)

    def moved(value, steps):
        pairs = [(i, (i + steps) % count) for i in range(count)]
        return lax.ppermute(value, "wide", pairs)

    def swapped(value):
        return lax.ppermute(value, "wide", [(i, i ^ 1) for i in range(count)])

    kv, q, u, spread = project(place, events, in_gain, w_uvqk[:, 0, :], w_out, heads)
    q_sib = swapped(q)
    back1 = moved(kv, 2)
    back4 = moved(kv, 8)
    acc, starts = attend(place, lengths, q, q_sib, [(kv, 0)], weight=0)
    w_half = lax.all_to_all(spread, "narrow", 0, 0)
    back1, acc = lax.optimization_barrier((back1, acc))
    back2 = moved(back1, 2)
    back3 = moved(back4, -2)
    acc = attend(place, lengths, q, q_sib, [(back1, 2), (back4, 8)], (starts, acc), weight=0)[0]
    acc = attend(place, lengths, q, q_sib, [(back2, 4)], (starts, acc), weight=50)[0]
    own, sib = attend(place, lengths, q, q_sib, [(back3, 6)], (starts, acc), weight=50, last=True)
    gated = gate(own, swapped(sib), u, out_gain)
    w_half, gated = lax.optimization_barrier((w_half, gated))
    w_other = swapped(w_half)
    gated = lax.all_to_all(gated.reshape(heads, rows // heads, DH), "narrow", 0, 0)
    out = combine(place, gated, w_half, w_other, events)
    return lax.all_to_all(out, "narrow", 0, 0).reshape(rows, DH)


def solution(mesh):
    in_specs = (
        P("wide", None),
        P(),
        P(),
        P(None, "narrow", None),
        P("narrow", None),
        P("narrow", None, None),
    )
    out_specs = P("wide", "narrow")
    return jax.shard_map(
        on_device, mesh=mesh, in_specs=in_specs, out_specs=out_specs, check_vma=False
    )
```

```python
import functools

import jax
import jax.numpy as jnp
from jax import lax
from jax.experimental import pallas as pl
from jax.experimental.pallas import tpu as pltpu
from jax.sharding import PartitionSpec as P

F32 = jnp.float32
BF16 = jnp.bfloat16
SMEM = pl.BlockSpec(memory_space=pltpu.SMEM)
VMEM = pl.BlockSpec(memory_space=pltpu.VMEM)
ROWS = 1024
DH = 128
HALF = 512
TQ = 512
TK = 256
NT = (((1,), (1,)), ((), ()))


def silu(x):
    half = 0.5 * x
    return half + half * jnp.tanh(half)


def kept(*values):
    return [pltpu.with_memory_space_constraint(value, pltpu.VMEM) for value in values]


def project_kernel(
    parts, place_ref, events_hbm, gain_hbm, w_hbm, w_out_hbm, kv_hbm, q_ref, u_hbm, spread_hbm,
    events, gain, w, w_half, kv_ref, u_ref, sems, out_sems, spread_sems,
):
    rows = events.shape[0] // parts
    fetch_w = pltpu.make_async_copy(w_hbm, w, sems.at[parts])
    fetch_gain = pltpu.make_async_copy(gain_hbm, gain, sems.at[parts + 1])
    fetches = [
        pltpu.make_async_copy(
            events_hbm.at[pl.ds(part * rows, rows)], events.at[pl.ds(part * rows, rows)], sems.at[part]
        )
        for part in range(parts)
    ]
    half = w_half.shape[1]
    columns = pl.ds(pl.multiple_of(place_ref[0] % 2 * half, half), half)
    fetch_half = pltpu.make_async_copy(w_out_hbm.at[0, :, columns], w_half, sems.at[parts + 2])
    fetches[0].start()
    fetch_gain.start()
    fetch_w.start()
    for fetch in fetches[1:]:
        fetch.start()
    fetch_half.start()
    stores = []
    for part in range(parts):
        fetches[part].wait()
        x = events[part * rows : (part + 1) * rows, :].astype(F32)
        average = jnp.mean(x, axis=-1, keepdims=True)
        centred = x - average
        variance = jnp.mean(centred * centred, axis=-1, keepdims=True)
        if part == 0:
            fetch_gain.wait()
        normed = (centred * lax.rsqrt(variance + 1e-05) * gain[...]).astype(BF16)
        if part == 0:
            fetch_w.wait()
        out = silu(jnp.dot(normed, w[...], preferred_element_type=F32)).astype(BF16)
        at = slice(part * rows, (part + 1) * rows)
        u_ref[at, :] = out[:, :DH]
        q_ref[at, :] = out[:, 2 * DH : 3 * DH]
        keys, values = out[:, 3 * DH :], out[:, DH : 2 * DH]
        kv_ref[at, :DH] = keys
        kv_ref[at, DH:] = values
        at = pl.ds(part * rows, rows)
        for index, (value_ref, value_hbm) in enumerate(((kv_ref, kv_hbm), (u_ref, u_hbm))):
            store = pltpu.make_async_copy(value_ref.at[at], value_hbm.at[at], out_sems.at[part, index])
            store.start()
            stores.append(store)
        if part == 0:
            fetch_half.wait()
            for copy in range(spread_hbm.shape[0]):
                store = pltpu.make_async_copy(w_half, spread_hbm.at[copy], spread_sems.at[copy])
                store.start()
                stores.append(store)
    for store in stores:
        store.wait()


def project(place, events, in_gain, w, w_out, copies):
    rows, width = events.shape
    parts = 4
    hbm = pl.BlockSpec(memory_space=pltpu.HBM)
    return pl.pallas_call(
        functools.partial(project_kernel, parts),
        in_specs=[SMEM] + [hbm] * 4,
        out_specs=[hbm, VMEM, hbm, hbm],
        out_shape=[
            pltpu.HBM((rows, 2 * DH), BF16),
            pltpu.VMEM((rows, DH), BF16),
            pltpu.HBM((rows, DH), BF16),
            pltpu.HBM((copies, DH, width // 2), BF16),
        ],
        scratch_shapes=[
            pltpu.VMEM((rows, width), BF16),
            pltpu.VMEM((1, width), F32),
            pltpu.VMEM((width, 4 * DH), BF16),
            pltpu.VMEM((DH, width // 2), BF16),
            pltpu.VMEM((rows, 2 * DH), BF16),
            pltpu.VMEM((rows, DH), BF16),
            pltpu.SemaphoreType.DMA((parts + 3,)),
            pltpu.SemaphoreType.DMA((parts, 2)),
            pltpu.SemaphoreType.DMA((copies,)),
        ],
        cost_estimate=pl.CostEstimate(
            flops=2 * rows * width * 4 * DH, bytes_accessed=4 << 20, transcendentals=rows * 4 * DH
        ),
        compiler_params=pltpu.CompilerParams(vmem_limit_bytes=20 << 20),
        name="project",
    )(
        place,
        *[pltpu.with_memory_space_constraint(value, pltpu.HBM) for value in (events, in_gain[None], w, w_out)],
    )


def attend_kernel(users, pieces, count, first, last, place_ref, lengths_ref, q_own, q_sib, *refs):
    blocks, refs = refs[:count], refs[count:]
    if first:
        total_out, starts_ref, q_ref, total_ref = refs
        outs = [total_out]
    else:
        starts_ref, carried = refs[:2]
        outs, (q_ref, total_ref) = refs[2:-2], refs[-2:]
    me = place_ref[0]
    scale = 0.5 * DH ** (-0.5)

    def weigh(scores):
        half = scores * scale
        return half + half * jnp.tanh(half)

    q_ref[:ROWS, :] = q_own[...]
    q_ref[ROWS:, :] = q_sib[...]
    if first:
        total_ref[...] = jnp.zeros_like(total_ref)
    else:
        total_ref[...] = carried[...]

    def one_part(part, nothing):
        side, inner = part // (ROWS // TQ), part % (ROWS // TQ)
        q_first = jnp.where(side == 0, me, me + 1 - 2 * (me % 2)) * ROWS + inner * TQ
        q_last = q_first + TQ - 1
        rows = pl.ds(pl.multiple_of(part * TQ, TQ), TQ)
        end = jnp.int32(0)
        low = jnp.int32(0)
        high = jnp.int32(0)
        for user in range(users):
            end = end + lengths_ref[user]
            low = jnp.where(end <= q_first, end, low)
            high = jnp.where(end <= q_last, end, high)
        if first:
            starts_ref[rows, :] = jnp.full((TQ, DH), low, jnp.int32)
            end = jnp.int32(0)
            for user in range(users):
                end = end + lengths_ref[user]

                @pl.when((end > q_first) & (end <= q_last))
                def _(end=end):
                    after = q_first + lax.broadcasted_iota(jnp.int32, (TQ, DH), 0) >= end
                    starts_ref[rows, :] = jnp.where(after, end, starts_ref[rows, :])

        for block, offset, back in pieces:
            kv_ref = blocks[block]
            k_first = (me - back) * ROWS + offset
            reached = (me >= back) & (k_first + HALF > low) & (k_first <= q_last)
            whole = (k_first >= high) & (k_first + HALF - 1 <= q_first)

            @pl.when(reached & whole)
            def _():
                q = q_ref[rows, :]
                weights = []
                for piece in range(HALF // TK):
                    keys = kv_ref[offset + piece * TK : offset + (piece + 1) * TK, :DH]
                    scores = lax.dot_general(q, keys, NT, preferred_element_type=F32)
                    weights.append(weigh(scores).astype(BF16))
                values = kv_ref[offset : offset + HALF, DH:]
                total_ref[rows, :] += jnp.dot(
                    jnp.concatenate(weights, axis=1), values, preferred_element_type=F32
                )

            @pl.when(reached & jnp.logical_not(whole))
            def _():
                q = q_ref[rows, :]
                begin = jnp.maximum(low - k_first, 0) // TK
                stop = jnp.minimum((q_last - k_first) // TK + 1, HALF // TK)
                q_start = starts_ref[rows, :]
                q_pos = q_first + lax.broadcasted_iota(jnp.int32, (TQ, DH), 0)

                def step(piece, carry):
                    at = pl.multiple_of(offset + piece * TK, TK)
                    keys = kv_ref[pl.ds(at, TK), :DH]
                    values = kv_ref[pl.ds(at, TK), DH:]
                    scores = lax.dot_general(q, keys, NT, preferred_element_type=F32)
                    lanes = lax.broadcasted_iota(jnp.int32, (TQ, DH), 1) + (k_first + piece * TK)
                    allowed = []
                    for strip in range(TK // DH):
                        k_pos = lanes + strip * DH
                        keep = (k_pos >= q_start) & (k_pos <= q_pos)
                        allowed.append(
                            jnp.where(keep, weigh(scores[:, strip * DH : (strip + 1) * DH]), 0.0)
                        )
                    weights = jnp.concatenate(allowed, axis=1).astype(BF16)
                    total_ref[rows, :] += jnp.dot(weights, values, preferred_element_type=F32)
                    return carry

                lax.fori_loop(begin, stop, step, 0)

        return nothing

    lax.fori_loop(0, 2 * ROWS // TQ, one_part, 0)
    if last:
        outs[0][...] = total_ref[:ROWS, :]
        outs[1][...] = total_ref[ROWS:, :].astype(BF16)
    else:
        outs[0][...] = total_ref[...]


def attend(place, lengths, q_own, q_sib, blocks, carried=None, weight=1, last=False):
    count = len(blocks)
    first = carried is None
    pieces = [
        (index, offset, back)
        for index, (block, back) in enumerate(blocks)
        for offset in range(0, block.shape[0], HALF)
    ]
    if first:
        outs = [
            pltpu.VMEM((2 * ROWS, DH), F32),
            pltpu.VMEM((2 * ROWS, DH), jnp.int32),
        ]
    elif last:
        outs = [pltpu.VMEM((ROWS, DH), F32), pltpu.VMEM((ROWS, DH), BF16)]
    else:
        outs = [pltpu.VMEM((2 * ROWS, DH), F32)]
    arrays = kept(q_own, q_sib, *[block[0] for block in blocks], *(() if first else carried))
    specs = [SMEM, SMEM] + [VMEM] * len(arrays)
    scratch = [pltpu.VMEM((2 * ROWS, DH), BF16), pltpu.VMEM((2 * ROWS, DH), F32)]
    return pl.pallas_call(
        functools.partial(attend_kernel, lengths.shape[0], pieces, count, first, last),
        in_specs=specs,
        out_specs=[VMEM] * len(outs),
        out_shape=outs,
        scratch_shapes=scratch,
        compiler_params=pltpu.CompilerParams(vmem_limit_bytes=20 << 20),
        cost_estimate=pl.CostEstimate(
            flops=weight * len(pieces) * 4 * ROWS * ROWS * DH,
            bytes_accessed=4 << 20,
            transcendentals=weight * len(pieces) * ROWS * ROWS,
        ),
        name="attend",
    )(place, lengths, *arrays)


def gate_kernel(own_ref, sib_ref, u_ref, gain_ref, out_ref):
    attended = own_ref[...] + sib_ref[...].astype(F32)
    centre = jnp.mean(attended, axis=-1, keepdims=True)
    centred = attended - centre
    deviation = jnp.mean(centred * centred, axis=-1, keepdims=True)
    gated = centred * lax.rsqrt(deviation + 1e-05) * gain_ref[...] * u_ref[...].astype(F32)
    out_ref[...] = gated.astype(BF16)


def gate(own, sib, u, gain):
    return pl.pallas_call(
        gate_kernel,
        in_specs=[VMEM] * 4,
        out_specs=VMEM,
        out_shape=pltpu.VMEM(u.shape, BF16),
        compiler_params=pltpu.CompilerParams(vmem_limit_bytes=8 << 20),
        name="gate",
    )(*kept(own, sib), u, gain)


def combine_kernel(heads, place_ref, gated_ref, mine_ref, other_ref, events_hbm, out_ref, events, sem):
    share = events.shape[0]
    fetch = pltpu.make_async_copy(
        events_hbm.at[pl.ds(pl.multiple_of(place_ref[1] * share, share), share)], events, sem
    )
    fetch.start()
    gated = jnp.concatenate([gated_ref[head] for head in range(heads)], axis=1)
    half = heads // 2
    core = place_ref[0] % 2
    totals = [
        jnp.dot(gated, w_ref[...].reshape(heads * DH, half * DH), preferred_element_type=F32)
        for w_ref in (mine_ref, other_ref)
    ]
    fetch.wait()
    for total, side in zip(totals, (core, 1 - core)):
        columns = pl.ds(pl.multiple_of(side * half * DH, half * DH), half * DH)
        total = (total + events[:, columns].astype(F32)).astype(BF16)
        for part in range(half):
            out_ref[side * half + part] = total[:, part * DH : (part + 1) * DH]


def combine(place, gated, mine, other, events):
    heads, share = gated.shape[:2]
    return pl.pallas_call(
        functools.partial(combine_kernel, heads),
        in_specs=[SMEM] + [VMEM] * 3 + [pl.BlockSpec(memory_space=pltpu.HBM)],
        out_specs=VMEM,
        out_shape=pltpu.VMEM(gated.shape, BF16),
        scratch_shapes=[pltpu.VMEM((share, events.shape[1]), BF16), pltpu.SemaphoreType.DMA],
        compiler_params=pltpu.CompilerParams(vmem_limit_bytes=8 << 20),
        name="combine",
    )(place, *kept(gated, mine, other), pltpu.with_memory_space_constraint(events, pltpu.HBM))


def on_device(events, lengths, in_gain, w_uvqk, out_gain, w_out):
    rows = events.shape[0]
    heads = lax.axis_size("narrow")
    count = lax.axis_size("wide")
    place = jnp.stack([lax.axis_index("wide"), lax.axis_index("narrow")]).astype(jnp.int32)

    def moved(value, steps):
        pairs = [(i, (i + steps) % count) for i in range(count)]
        return lax.ppermute(value, "wide", pairs)

    def swapped(value):
        return lax.ppermute(value, "wide", [(i, i ^ 1) for i in range(count)])

    kv, q, u, spread = project(place, events, in_gain, w_uvqk[:, 0, :], w_out, heads)
    q_sib = swapped(q)
    back1 = moved(kv, 2)
    back4 = moved(kv, 8)
    acc, starts = attend(place, lengths, q, q_sib, [(kv, 0)], weight=0)
    w_half = lax.all_to_all(spread, "narrow", 0, 0)
    back1, acc = lax.optimization_barrier((back1, acc))
    back2 = moved(back1, 2)
    back3 = moved(back4, -2)
    acc = attend(place, lengths, q, q_sib, [(back1, 2), (back4, 8)], (starts, acc), weight=50)[0]
    acc = attend(place, lengths, q, q_sib, [(back2, 4)], (starts, acc), weight=50)[0]
    own, sib = attend(place, lengths, q, q_sib, [(back3, 6)], (starts, acc), weight=50, last=True)
    gated = gate(own, swapped(sib), u, out_gain)
    w_half, gated = lax.optimization_barrier((w_half, gated))
    w_other = swapped(w_half)
    gated = lax.all_to_all(gated.reshape(heads, rows // heads, DH), "narrow", 0, 0)
    out = combine(place, gated, w_half, w_other, events)
    return lax.all_to_all(out, "narrow", 0, 0).reshape(rows, DH)


def solution(mesh):
    in_specs = (
        P("wide", None),
        P(),
        P(),
        P(None, "narrow", None),
        P("narrow", None),
        P("narrow", None, None),
    )
    out_specs = P("wide", "narrow")
    return jax.shard_map(
        on_device, mesh=mesh, in_specs=in_specs, out_specs=out_specs, check_vma=False
    )
```

```python
import functools

import jax
import jax.numpy as jnp
from jax import lax
from jax.experimental import pallas as pl
from jax.experimental.pallas import tpu as pltpu
from jax.sharding import PartitionSpec as P

F32 = jnp.float32
BF16 = jnp.bfloat16
SMEM = pl.BlockSpec(memory_space=pltpu.SMEM)
VMEM = pl.BlockSpec(memory_space=pltpu.VMEM)
ROWS = 1024
DH = 128
HALF = 512
TQ = 512
TK = 256
NT = (((1,), (1,)), ((), ()))


def silu(x):
    half = 0.5 * x
    return half + half * jnp.tanh(half)


def kept(*values):
    return [pltpu.with_memory_space_constraint(value, pltpu.VMEM) for value in values]


def project_kernel(
    parts, place_ref, events_hbm, gain_hbm, w_hbm, w_out_hbm, kv_hbm, q_ref, u_hbm, spread_hbm,
    events, gain, w, w_half, kv_ref, u_ref, sems, out_sems, spread_sems,
):
    rows = events.shape[0] // parts
    fetch_w = pltpu.make_async_copy(w_hbm, w, sems.at[parts])
    fetch_gain = pltpu.make_async_copy(gain_hbm, gain, sems.at[parts + 1])
    fetches = [
        pltpu.make_async_copy(
            events_hbm.at[pl.ds(part * rows, rows)], events.at[pl.ds(part * rows, rows)], sems.at[part]
        )
        for part in range(parts)
    ]
    half = w_half.shape[1]
    columns = pl.ds(pl.multiple_of(place_ref[0] % 2 * half, half), half)
    fetch_half = pltpu.make_async_copy(w_out_hbm.at[0, :, columns], w_half, sems.at[parts + 2])
    fetches[0].start()
    fetch_gain.start()
    fetch_w.start()
    for fetch in fetches[1:]:
        fetch.start()
    fetch_half.start()
    stores = []
    for part in range(parts):
        fetches[part].wait()
        x = events[part * rows : (part + 1) * rows, :].astype(F32)
        average = jnp.mean(x, axis=-1, keepdims=True)
        centred = x - average
        variance = jnp.mean(centred * centred, axis=-1, keepdims=True)
        if part == 0:
            fetch_gain.wait()
        normed = (centred * lax.rsqrt(variance + 1e-05) * gain[...]).astype(BF16)
        if part == 0:
            fetch_w.wait()
        out = silu(jnp.dot(normed, w[...], preferred_element_type=F32)).astype(BF16)
        at = slice(part * rows, (part + 1) * rows)
        u_ref[at, :] = out[:, :DH]
        q_ref[at, :] = out[:, 2 * DH : 3 * DH]
        keys, values = out[:, 3 * DH :], out[:, DH : 2 * DH]
        kv_ref[at, :DH] = keys
        kv_ref[at, DH:] = values
        at = pl.ds(part * rows, rows)
        for index, (value_ref, value_hbm) in enumerate(((kv_ref, kv_hbm), (u_ref, u_hbm))):
            store = pltpu.make_async_copy(value_ref.at[at], value_hbm.at[at], out_sems.at[part, index])
            store.start()
            stores.append(store)
        if part == 0:
            fetch_half.wait()
            for copy in range(spread_hbm.shape[0]):
                store = pltpu.make_async_copy(w_half, spread_hbm.at[copy], spread_sems.at[copy])
                store.start()
                stores.append(store)
    for store in stores:
        store.wait()


def project(place, events, in_gain, w, w_out, copies):
    rows, width = events.shape
    parts = 4
    hbm = pl.BlockSpec(memory_space=pltpu.HBM)
    return pl.pallas_call(
        functools.partial(project_kernel, parts),
        in_specs=[SMEM] + [hbm] * 4,
        out_specs=[hbm, VMEM, hbm, hbm],
        out_shape=[
            pltpu.HBM((rows, 2 * DH), BF16),
            pltpu.VMEM((rows, DH), BF16),
            pltpu.HBM((rows, DH), BF16),
            pltpu.HBM((copies, DH, width // 2), BF16),
        ],
        scratch_shapes=[
            pltpu.VMEM((rows, width), BF16),
            pltpu.VMEM((1, width), F32),
            pltpu.VMEM((width, 4 * DH), BF16),
            pltpu.VMEM((DH, width // 2), BF16),
            pltpu.VMEM((rows, 2 * DH), BF16),
            pltpu.VMEM((rows, DH), BF16),
            pltpu.SemaphoreType.DMA((parts + 3,)),
            pltpu.SemaphoreType.DMA((parts, 2)),
            pltpu.SemaphoreType.DMA((copies,)),
        ],
        cost_estimate=pl.CostEstimate(
            flops=2 * rows * width * 4 * DH, bytes_accessed=4 << 20, transcendentals=rows * 4 * DH
        ),
        compiler_params=pltpu.CompilerParams(vmem_limit_bytes=20 << 20),
        name="project",
    )(
        place,
        *[pltpu.with_memory_space_constraint(value, pltpu.HBM) for value in (events, in_gain[None], w, w_out)],
    )


def attend_kernel(users, pieces, count, first, last, place_ref, lengths_ref, q_own, q_sib, *refs):
    blocks, refs = refs[:count], refs[count:]
    if first:
        total_out, starts_ref, q_ref, total_ref = refs
        outs = [total_out]
    else:
        starts_ref, carried = refs[:2]
        outs, (q_ref, total_ref) = refs[2:-2], refs[-2:]
    me = place_ref[0]
    scale = 0.5 * DH ** (-0.5)

    def weigh(scores):
        half = scores * scale
        return half + half * jnp.tanh(half)

    q_ref[:ROWS, :] = q_own[...]
    q_ref[ROWS:, :] = q_sib[...]
    if first:
        total_ref[...] = jnp.zeros_like(total_ref)
    else:
        total_ref[...] = carried[...]

    def add_whole(kv_ref, offset, rows):
        q = q_ref[rows, :]
        weights = []
        for piece in range(HALF // TK):
            keys = kv_ref[offset + piece * TK : offset + (piece + 1) * TK, :DH]
            scores = lax.dot_general(q, keys, NT, preferred_element_type=F32)
            weights.append(weigh(scores).astype(BF16))
        values = kv_ref[offset : offset + HALF, DH:]
        total_ref[rows, :] += jnp.dot(
            jnp.concatenate(weights, axis=1), values, preferred_element_type=F32
        )

    def add_masked(kv_ref, offset, rows, k_first, q_first, low):
        q = q_ref[rows, :]
        begin = jnp.maximum(low - k_first, 0) // TK
        stop = jnp.minimum((q_first + TQ - 1 - k_first) // TK + 1, HALF // TK)
        q_start = starts_ref[rows, :]
        q_pos = q_first + lax.broadcasted_iota(jnp.int32, (TQ, DH), 0)

        def step(piece, carry):
            at = pl.multiple_of(offset + piece * TK, TK)
            keys = kv_ref[pl.ds(at, TK), :DH]
            values = kv_ref[pl.ds(at, TK), DH:]
            scores = lax.dot_general(q, keys, NT, preferred_element_type=F32)
            lanes = lax.broadcasted_iota(jnp.int32, (TQ, DH), 1) + (k_first + piece * TK)
            allowed = []
            for strip in range(TK // DH):
                k_pos = lanes + strip * DH
                keep = (k_pos >= q_start) & (k_pos <= q_pos)
                allowed.append(jnp.where(keep, weigh(scores[:, strip * DH : (strip + 1) * DH]), 0.0))
            weights = jnp.concatenate(allowed, axis=1).astype(BF16)
            total_ref[rows, :] += jnp.dot(weights, values, preferred_element_type=F32)
            return carry

        lax.fori_loop(begin, stop, step, 0)

    def one_side(side, nothing):
        side_first = jnp.where(side == 0, me, me + 1 - 2 * (me % 2)) * ROWS
        parts = []
        for inner in range(ROWS // TQ):
            q_first = side_first + inner * TQ
            q_last = q_first + TQ - 1
            rows = pl.ds(pl.multiple_of(side * ROWS + inner * TQ, TQ), TQ)
            end = jnp.int32(0)
            low = jnp.int32(0)
            high = jnp.int32(0)
            for user in range(users):
                end = end + lengths_ref[user]
                low = jnp.where(end <= q_first, end, low)
                high = jnp.where(end <= q_last, end, high)
            parts.append((q_first, q_last, rows, low, high))
            if first:
                starts_ref[rows, :] = jnp.full((TQ, DH), low, jnp.int32)
                end = jnp.int32(0)
                for user in range(users):
                    end = end + lengths_ref[user]

                    @pl.when((end > q_first) & (end <= q_last))
                    def _(end=end, q_first=q_first, rows=rows):
                        after = q_first + lax.broadcasted_iota(jnp.int32, (TQ, DH), 0) >= end
                        starts_ref[rows, :] = jnp.where(after, end, starts_ref[rows, :])

        for block, offset, back in pieces:
            kv_ref = blocks[block]
            k_first = (me - back) * ROWS + offset
            there = me >= back
            alike = there & (k_first >= parts[-1][4]) & (k_first + HALF - 1 <= side_first)

            @pl.when(alike)
            def _(kv_ref=kv_ref, offset=offset):
                add_whole(kv_ref, offset, pl.ds(pl.multiple_of(side * ROWS, ROWS), ROWS))

            @pl.when(jnp.logical_not(alike))
            def _(kv_ref=kv_ref, offset=offset, k_first=k_first, there=there):
                for q_first, q_last, rows, low, high in parts:
                    reached = there & (k_first + HALF > low) & (k_first <= q_last)
                    whole = (k_first >= high) & (k_first + HALF - 1 <= q_first)

                    @pl.when(reached & whole)
                    def _(rows=rows):
                        add_whole(kv_ref, offset, rows)

                    @pl.when(reached & jnp.logical_not(whole))
                    def _(rows=rows, q_first=q_first, low=low):
                        add_masked(kv_ref, offset, rows, k_first, q_first, low)

        return nothing

    lax.fori_loop(0, 2, one_side, 0)
    if last:
        outs[0][...] = total_ref[:ROWS, :]
        outs[1][...] = total_ref[ROWS:, :].astype(BF16)
    else:
        outs[0][...] = total_ref[...]


def attend(place, lengths, q_own, q_sib, blocks, carried=None, weight=1, last=False):
    count = len(blocks)
    first = carried is None
    pieces = [
        (index, offset, back)
        for index, (block, back) in enumerate(blocks)
        for offset in range(0, block.shape[0], HALF)
    ]
    if first:
        outs = [
            pltpu.VMEM((2 * ROWS, DH), F32),
            pltpu.VMEM((2 * ROWS, DH), jnp.int32),
        ]
    elif last:
        outs = [pltpu.VMEM((ROWS, DH), F32), pltpu.VMEM((ROWS, DH), BF16)]
    else:
        outs = [pltpu.VMEM((2 * ROWS, DH), F32)]
    arrays = kept(q_own, q_sib, *[block[0] for block in blocks], *(() if first else carried))
    specs = [SMEM, SMEM] + [VMEM] * len(arrays)
    scratch = [pltpu.VMEM((2 * ROWS, DH), BF16), pltpu.VMEM((2 * ROWS, DH), F32)]
    return pl.pallas_call(
        functools.partial(attend_kernel, lengths.shape[0], pieces, count, first, last),
        in_specs=specs,
        out_specs=[VMEM] * len(outs),
        out_shape=outs,
        scratch_shapes=scratch,
        compiler_params=pltpu.CompilerParams(vmem_limit_bytes=20 << 20),
        cost_estimate=pl.CostEstimate(
            flops=weight * len(pieces) * 4 * ROWS * ROWS * DH,
            bytes_accessed=4 << 20,
            transcendentals=weight * len(pieces) * ROWS * ROWS,
        ),
        name="attend",
    )(place, lengths, *arrays)


def gate_kernel(own_ref, sib_ref, u_ref, gain_ref, out_ref):
    attended = own_ref[...] + sib_ref[...].astype(F32)
    centre = jnp.mean(attended, axis=-1, keepdims=True)
    centred = attended - centre
    deviation = jnp.mean(centred * centred, axis=-1, keepdims=True)
    gated = centred * lax.rsqrt(deviation + 1e-05) * gain_ref[...] * u_ref[...].astype(F32)
    out_ref[...] = gated.astype(BF16)


def gate(own, sib, u, gain):
    return pl.pallas_call(
        gate_kernel,
        in_specs=[VMEM] * 4,
        out_specs=VMEM,
        out_shape=pltpu.VMEM(u.shape, BF16),
        compiler_params=pltpu.CompilerParams(vmem_limit_bytes=8 << 20),
        name="gate",
    )(*kept(own, sib), u, gain)


def combine_kernel(heads, place_ref, gated_ref, mine_ref, other_ref, events_hbm, out_ref, events, sem):
    share = events.shape[0]
    fetch = pltpu.make_async_copy(
        events_hbm.at[pl.ds(pl.multiple_of(place_ref[1] * share, share), share)], events, sem
    )
    fetch.start()
    gated = jnp.concatenate([gated_ref[head] for head in range(heads)], axis=1)
    half = heads // 2
    core = place_ref[0] % 2
    totals = [
        jnp.dot(gated, w_ref[...].reshape(heads * DH, half * DH), preferred_element_type=F32)
        for w_ref in (mine_ref, other_ref)
    ]
    fetch.wait()
    for total, side in zip(totals, (core, 1 - core)):
        columns = pl.ds(pl.multiple_of(side * half * DH, half * DH), half * DH)
        total = (total + events[:, columns].astype(F32)).astype(BF16)
        for part in range(half):
            out_ref[side * half + part] = total[:, part * DH : (part + 1) * DH]


def combine(place, gated, mine, other, events):
    heads, share = gated.shape[:2]
    return pl.pallas_call(
        functools.partial(combine_kernel, heads),
        in_specs=[SMEM] + [VMEM] * 3 + [pl.BlockSpec(memory_space=pltpu.HBM)],
        out_specs=VMEM,
        out_shape=pltpu.VMEM(gated.shape, BF16),
        scratch_shapes=[pltpu.VMEM((share, events.shape[1]), BF16), pltpu.SemaphoreType.DMA],
        compiler_params=pltpu.CompilerParams(vmem_limit_bytes=8 << 20),
        name="combine",
    )(place, *kept(gated, mine, other), pltpu.with_memory_space_constraint(events, pltpu.HBM))


def on_device(events, lengths, in_gain, w_uvqk, out_gain, w_out):
    rows = events.shape[0]
    heads = lax.axis_size("narrow")
    count = lax.axis_size("wide")
    place = jnp.stack([lax.axis_index("wide"), lax.axis_index("narrow")]).astype(jnp.int32)

    def moved(value, steps):
        pairs = [(i, (i + steps) % count) for i in range(count)]
        return lax.ppermute(value, "wide", pairs)

    def swapped(value):
        return lax.ppermute(value, "wide", [(i, i ^ 1) for i in range(count)])

    kv, q, u, spread = project(place, events, in_gain, w_uvqk[:, 0, :], w_out, heads)
    q_sib = swapped(q)
    back1 = moved(kv, 2)
    back4 = moved(kv, 8)
    acc, starts = attend(place, lengths, q, q_sib, [(kv, 0)], weight=0)
    w_half = lax.all_to_all(spread, "narrow", 0, 0)
    back1, acc = lax.optimization_barrier((back1, acc))
    back2 = moved(back1, 2)
    back3 = moved(back4, -2)
    acc = attend(place, lengths, q, q_sib, [(back1, 2), (back4, 8)], (starts, acc), weight=50)[0]
    acc = attend(place, lengths, q, q_sib, [(back2, 4)], (starts, acc), weight=50)[0]
    own, sib = attend(place, lengths, q, q_sib, [(back3, 6)], (starts, acc), weight=50, last=True)
    gated = gate(own, swapped(sib), u, out_gain)
    w_half, gated = lax.optimization_barrier((w_half, gated))
    w_other = swapped(w_half)
    gated = lax.all_to_all(gated.reshape(heads, rows // heads, DH), "narrow", 0, 0)
    out = combine(place, gated, w_half, w_other, events)
    return lax.all_to_all(out, "narrow", 0, 0).reshape(rows, DH)


def solution(mesh):
    in_specs = (
        P("wide", None),
        P(),
        P(),
        P(None, "narrow", None),
        P("narrow", None),
        P("narrow", None, None),
    )
    out_specs = P("wide", "narrow")
    return jax.shard_map(
        on_device, mesh=mesh, in_specs=in_specs, out_specs=out_specs, check_vma=False
    )
```

```python
import functools

import jax
import jax.numpy as jnp
from jax import lax
from jax.experimental import pallas as pl
from jax.experimental.pallas import tpu as pltpu
from jax.sharding import PartitionSpec as P

F32 = jnp.float32
BF16 = jnp.bfloat16
SMEM = pl.BlockSpec(memory_space=pltpu.SMEM)
VMEM = pl.BlockSpec(memory_space=pltpu.VMEM)
ROWS = 1024
DH = 128
HALF = 512
TQ = 512
TK = 256
NT = (((1,), (1,)), ((), ()))


def silu(x):
    half = 0.5 * x
    return half + half * jnp.tanh(half)


def kept(*values):
    return [pltpu.with_memory_space_constraint(value, pltpu.VMEM) for value in values]


def project_kernel(
    parts, place_ref, events_hbm, gain_hbm, w_hbm, w_out_hbm, kv_hbm, q_ref, u_hbm, spread_hbm,
    events, gain, w, w_half, kv_ref, u_ref, sems, out_sems, spread_sems,
):
    rows = events.shape[0] // parts
    fetch_w = pltpu.make_async_copy(w_hbm, w, sems.at[parts])
    fetch_gain = pltpu.make_async_copy(gain_hbm, gain, sems.at[parts + 1])
    fetches = [
        pltpu.make_async_copy(
            events_hbm.at[pl.ds(part * rows, rows)], events.at[pl.ds(part * rows, rows)], sems.at[part]
        )
        for part in range(parts)
    ]
    half = w_half.shape[1]
    columns = pl.ds(pl.multiple_of(place_ref[0] % 2 * half, half), half)
    fetch_half = pltpu.make_async_copy(w_out_hbm.at[0, :, columns], w_half, sems.at[parts + 2])
    fetches[0].start()
    fetch_gain.start()
    fetch_w.start()
    for fetch in fetches[1:]:
        fetch.start()
    fetch_half.start()
    stores = []
    for part in range(parts):
        fetches[part].wait()
        x = events[part * rows : (part + 1) * rows, :].astype(F32)
        average = jnp.mean(x, axis=-1, keepdims=True)
        centred = x - average
        variance = jnp.mean(centred * centred, axis=-1, keepdims=True)
        if part == 0:
            fetch_gain.wait()
        normed = (centred * lax.rsqrt(variance + 1e-05) * gain[...]).astype(BF16)
        if part == 0:
            fetch_w.wait()
        out = silu(jnp.dot(normed, w[...], preferred_element_type=F32)).astype(BF16)
        at = slice(part * rows, (part + 1) * rows)
        u_ref[at, :] = out[:, :DH]
        q_ref[at, :] = out[:, 2 * DH : 3 * DH]
        keys, values = out[:, 3 * DH :], out[:, DH : 2 * DH]
        kv_ref[at, :DH] = keys
        kv_ref[at, DH:] = values
        at = pl.ds(part * rows, rows)
        for index, (value_ref, value_hbm) in enumerate(((kv_ref, kv_hbm), (u_ref, u_hbm))):
            store = pltpu.make_async_copy(value_ref.at[at], value_hbm.at[at], out_sems.at[part, index])
            store.start()
            stores.append(store)
        if part == 0:
            fetch_half.wait()
            for copy in range(spread_hbm.shape[0]):
                store = pltpu.make_async_copy(w_half, spread_hbm.at[copy], spread_sems.at[copy])
                store.start()
                stores.append(store)
    for store in stores:
        store.wait()


def project(place, events, in_gain, w, w_out, copies):
    rows, width = events.shape
    parts = 4
    hbm = pl.BlockSpec(memory_space=pltpu.HBM)
    return pl.pallas_call(
        functools.partial(project_kernel, parts),
        in_specs=[SMEM] + [hbm] * 4,
        out_specs=[hbm, VMEM, hbm, hbm],
        out_shape=[
            pltpu.HBM((rows, 2 * DH), BF16),
            pltpu.VMEM((rows, DH), BF16),
            pltpu.HBM((rows, DH), BF16),
            pltpu.HBM((copies, DH, width // 2), BF16),
        ],
        scratch_shapes=[
            pltpu.VMEM((rows, width), BF16),
            pltpu.VMEM((1, width), F32),
            pltpu.VMEM((width, 4 * DH), BF16),
            pltpu.VMEM((DH, width // 2), BF16),
            pltpu.VMEM((rows, 2 * DH), BF16),
            pltpu.VMEM((rows, DH), BF16),
            pltpu.SemaphoreType.DMA((parts + 3,)),
            pltpu.SemaphoreType.DMA((parts, 2)),
            pltpu.SemaphoreType.DMA((copies,)),
        ],
        cost_estimate=pl.CostEstimate(
            flops=2 * rows * width * 4 * DH, bytes_accessed=4 << 20, transcendentals=rows * 4 * DH
        ),
        compiler_params=pltpu.CompilerParams(vmem_limit_bytes=20 << 20),
        name="project",
    )(
        place,
        *[pltpu.with_memory_space_constraint(value, pltpu.HBM) for value in (events, in_gain[None], w, w_out)],
    )


def attend_kernel(users, pieces, count, first, last, place_ref, lengths_ref, q_own, q_sib, *refs):
    blocks, refs = refs[:count], refs[count:]
    if first:
        total_out, starts_ref, q_ref, total_ref = refs
        outs = [total_out]
    else:
        starts_ref, carried = refs[:2]
        outs, (q_ref, total_ref) = refs[2:-2], refs[-2:]
    me = place_ref[0]
    scale = 0.5 * DH ** (-0.5)

    def weigh(scores):
        half = scores * scale
        return half + half * jnp.tanh(half)

    q_ref[:ROWS, :] = q_own[...]
    q_ref[ROWS:, :] = q_sib[...]
    if first:
        total_ref[...] = jnp.zeros_like(total_ref)
    else:
        total_ref[...] = carried[...]

    def add_whole(kv_ref, offset, rows):
        q = q_ref[rows, :]
        weights = []
        for piece in range(HALF // TK):
            keys = kv_ref[offset + piece * TK : offset + (piece + 1) * TK, :DH]
            scores = lax.dot_general(q, keys, NT, preferred_element_type=F32)
            weights.append(weigh(scores).astype(BF16))
        values = kv_ref[offset : offset + HALF, DH:]
        total_ref[rows, :] += jnp.dot(
            jnp.concatenate(weights, axis=1), values, preferred_element_type=F32
        )

    def add_masked(kv_ref, offset, rows, k_first, q_first, low):
        q = q_ref[rows, :]
        begin = jnp.maximum(low - k_first, 0) // TK
        stop = jnp.minimum((q_first + TQ - 1 - k_first) // TK + 1, HALF // TK)
        q_start = starts_ref[rows, :]
        q_pos = q_first + lax.broadcasted_iota(jnp.int32, (TQ, DH), 0)

        def step(piece, carry):
            at = pl.multiple_of(offset + piece * TK, TK)
            keys = kv_ref[pl.ds(at, TK), :DH]
            values = kv_ref[pl.ds(at, TK), DH:]
            scores = lax.dot_general(q, keys, NT, preferred_element_type=F32)
            lanes = lax.broadcasted_iota(jnp.int32, (TQ, DH), 1) + (k_first + piece * TK)
            allowed = []
            for strip in range(TK // DH):
                k_pos = lanes + strip * DH
                keep = (k_pos >= q_start) & (k_pos <= q_pos)
                allowed.append(jnp.where(keep, weigh(scores[:, strip * DH : (strip + 1) * DH]), 0.0))
            weights = jnp.concatenate(allowed, axis=1).astype(BF16)
            total_ref[rows, :] += jnp.dot(weights, values, preferred_element_type=F32)
            return carry

        lax.fori_loop(begin, stop, step, 0)

    def one_side(side, nothing):
        side_first = jnp.where(side == 0, me, me + 1 - 2 * (me % 2)) * ROWS
        parts = []
        for inner in range(ROWS // TQ):
            q_first = side_first + inner * TQ
            q_last = q_first + TQ - 1
            rows = pl.ds(pl.multiple_of(side * ROWS + inner * TQ, TQ), TQ)
            end = jnp.int32(0)
            low = jnp.int32(0)
            high = jnp.int32(0)
            for user in range(users):
                end = end + lengths_ref[user]
                low = jnp.where(end <= q_first, end, low)
                high = jnp.where(end <= q_last, end, high)
            parts.append((q_first, q_last, rows, low, high))
            if first:
                starts_ref[rows, :] = jnp.full((TQ, DH), low, jnp.int32)
                end = jnp.int32(0)
                for user in range(users):
                    end = end + lengths_ref[user]

                    @pl.when((end > q_first) & (end <= q_last))
                    def _(end=end, q_first=q_first, rows=rows):
                        after = q_first + lax.broadcasted_iota(jnp.int32, (TQ, DH), 0) >= end
                        starts_ref[rows, :] = jnp.where(after, end, starts_ref[rows, :])

        for block, offset, back in pieces:
            kv_ref = blocks[block]
            k_first = (me - back) * ROWS + offset
            there = me >= back
            alike = there & (k_first >= parts[-1][4]) & (k_first + HALF - 1 <= side_first)

            @pl.when(alike)
            def _(kv_ref=kv_ref, offset=offset):
                add_whole(kv_ref, offset, pl.ds(pl.multiple_of(side * ROWS, ROWS), ROWS))

            @pl.when(jnp.logical_not(alike))
            def _(kv_ref=kv_ref, offset=offset, k_first=k_first, there=there):
                for q_first, q_last, rows, low, high in parts:
                    reached = there & (k_first + HALF > low) & (k_first <= q_last)
                    whole = (k_first >= high) & (k_first + HALF - 1 <= q_first)

                    @pl.when(reached & whole)
                    def _(rows=rows):
                        add_whole(kv_ref, offset, rows)

                    @pl.when(reached & jnp.logical_not(whole))
                    def _(rows=rows, q_first=q_first, low=low):
                        add_masked(kv_ref, offset, rows, k_first, q_first, low)

        return nothing

    lax.fori_loop(0, 2, one_side, 0)
    if last:
        outs[0][...] = total_ref[:ROWS, :]
        outs[1][...] = total_ref[ROWS:, :].astype(BF16)
    else:
        outs[0][...] = total_ref[...]


def attend(place, lengths, q_own, q_sib, blocks, carried=None, weight=1, last=False):
    count = len(blocks)
    first = carried is None
    pieces = [
        (index, offset, back)
        for index, (block, back) in enumerate(blocks)
        for offset in range(0, block.shape[0], HALF)
    ]
    if first:
        outs = [
            pltpu.VMEM((2 * ROWS, DH), F32),
            pltpu.VMEM((2 * ROWS, DH), jnp.int32),
        ]
    elif last:
        outs = [pltpu.VMEM((ROWS, DH), F32), pltpu.VMEM((ROWS, DH), BF16)]
    else:
        outs = [pltpu.VMEM((2 * ROWS, DH), F32)]
    arrays = kept(q_own, q_sib, *[block[0] for block in blocks], *(() if first else carried))
    specs = [SMEM, SMEM] + [VMEM] * len(arrays)
    scratch = [pltpu.VMEM((2 * ROWS, DH), BF16), pltpu.VMEM((2 * ROWS, DH), F32)]
    return pl.pallas_call(
        functools.partial(attend_kernel, lengths.shape[0], pieces, count, first, last),
        in_specs=specs,
        out_specs=[VMEM] * len(outs),
        out_shape=outs,
        scratch_shapes=scratch,
        compiler_params=pltpu.CompilerParams(vmem_limit_bytes=20 << 20),
        cost_estimate=pl.CostEstimate(
            flops=weight * len(pieces) * 4 * ROWS * ROWS * DH,
            bytes_accessed=4 << 20,
            transcendentals=weight * len(pieces) * ROWS * ROWS,
        ),
        name="attend",
    )(place, lengths, *arrays)


def gate_kernel(shares, own_ref, sib_ref, u_ref, gain_ref, out_ref):
    attended = own_ref[...] + sib_ref[...].astype(F32)
    centre = jnp.mean(attended, axis=-1, keepdims=True)
    centred = attended - centre
    deviation = jnp.mean(centred * centred, axis=-1, keepdims=True)
    gated = centred * lax.rsqrt(deviation + 1e-05) * gain_ref[...] * u_ref[...].astype(F32)
    gated = gated.astype(BF16)
    share = gated.shape[0] // shares
    for part in range(shares):
        out_ref[shares - 1 - part] = gated[part * share : (part + 1) * share, :]


def gate(own, sib, u, gain, shares):
    return pl.pallas_call(
        functools.partial(gate_kernel, shares),
        in_specs=[VMEM] * 4,
        out_specs=VMEM,
        out_shape=pltpu.VMEM((shares, u.shape[0] // shares, DH), BF16),
        compiler_params=pltpu.CompilerParams(vmem_limit_bytes=8 << 20),
        name="gate",
    )(*kept(own, sib), u, gain)


def combine_kernel(heads, parts, place_ref, gated_ref, mine_hbm, other_hbm, events_hbm, out_ref, events, w, sems, sem):
    share = events.shape[0]
    deep = heads // parts
    half = heads // 2
    core = place_ref[0] % 2
    fetches = [
        [
            pltpu.make_async_copy(
                w_hbm.at[pl.ds(part * deep, deep)], w.at[index, pl.ds(part * deep, deep)], sems.at[index, part]
            )
            for part in range(parts)
        ]
        for index, w_hbm in enumerate((mine_hbm, other_hbm))
    ]
    first = pl.multiple_of(place_ref[1] * share, share)
    fetch_events = pltpu.make_async_copy(events_hbm.at[pl.ds(first, share)], events, sem)
    for fetch in fetches[0]:
        fetch.start()
    fetch_events.start()
    for fetch in fetches[1]:
        fetch.start()
    gated = jnp.concatenate([gated_ref[heads - 1 - head] for head in range(heads)], axis=1)
    for index, side in enumerate((core, 1 - core)):
        total = jnp.zeros((share, half * DH), F32)
        for part in range(parts):
            fetches[index][part].wait()
            rows = w[index, part * deep : (part + 1) * deep].reshape(deep * DH, half * DH)
            at = slice(part * deep * DH, (part + 1) * deep * DH)
            total += jnp.dot(gated[:, at], rows, preferred_element_type=F32)
        if index == 0:
            fetch_events.wait()
        columns = pl.ds(pl.multiple_of(side * half * DH, half * DH), half * DH)
        total = (total + events[:, columns].astype(F32)).astype(BF16)
        for part in range(half):
            out_ref[side * half + part] = total[:, part * DH : (part + 1) * DH]


def combine(place, gated, mine, other, events):
    heads, share = gated.shape[:2]
    parts = 4
    hbm = pl.BlockSpec(memory_space=pltpu.HBM)
    anywhere = pl.BlockSpec(memory_space=pl.ANY)
    return pl.pallas_call(
        functools.partial(combine_kernel, heads, parts),
        in_specs=[SMEM, VMEM, anywhere, anywhere, hbm],
        out_specs=VMEM,
        out_shape=pltpu.VMEM(gated.shape, BF16),
        scratch_shapes=[
            pltpu.VMEM((share, events.shape[1]), BF16),
            pltpu.VMEM((2,) + mine.shape, BF16),
            pltpu.SemaphoreType.DMA((2, parts)),
            pltpu.SemaphoreType.DMA,
        ],
        compiler_params=pltpu.CompilerParams(vmem_limit_bytes=8 << 20),
        name="combine",
    )(
        place,
        *kept(gated),
        mine,
        other,
        pltpu.with_memory_space_constraint(events, pltpu.HBM),
    )


def on_device(events, lengths, in_gain, w_uvqk, out_gain, w_out):
    rows = events.shape[0]
    heads = lax.axis_size("narrow")
    count = lax.axis_size("wide")
    place = jnp.stack([lax.axis_index("wide"), lax.axis_index("narrow")]).astype(jnp.int32)

    def moved(value, steps):
        pairs = [(i, (i + steps) % count) for i in range(count)]
        return lax.ppermute(value, "wide", pairs)

    def swapped(value):
        return lax.ppermute(value, "wide", [(i, i ^ 1) for i in range(count)])

    kv, q, u, spread = project(place, events, in_gain, w_uvqk[:, 0, :], w_out, heads)
    q_sib = swapped(q)
    back1 = moved(kv, 2)
    back4 = moved(kv, 8)
    acc, starts = attend(place, lengths, q, q_sib, [(kv, 0)], weight=0)
    w_half = lax.all_to_all(spread, "narrow", 0, 0)
    back1, acc = lax.optimization_barrier((back1, acc))
    back2 = moved(back1, 2)
    back3 = moved(back4, -2)
    acc = attend(place, lengths, q, q_sib, [(back1, 2), (back4, 8)], (starts, acc), weight=50)[0]
    acc = attend(place, lengths, q, q_sib, [(back2, 4)], (starts, acc), weight=50)[0]
    own, sib = attend(place, lengths, q, q_sib, [(back3, 6)], (starts, acc), weight=50, last=True)
    gated = gate(own, swapped(sib), u, out_gain, heads)
    w_half, gated = lax.optimization_barrier((w_half, gated))
    w_other = swapped(w_half)
    order = [list(range(heads))[::-1]]
    gated = lax.all_to_all(gated, "narrow", 0, 0, axis_index_groups=order)
    out = combine(place, gated, w_half, w_other, events)
    return lax.all_to_all(out, "narrow", 0, 0).reshape(rows, DH)


def solution(mesh):
    in_specs = (
        P("wide", None),
        P(),
        P(),
        P(None, "narrow", None),
        P("narrow", None),
        P("narrow", None, None),
    )
    out_specs = P("wide", "narrow")
    return jax.shard_map(
        on_device, mesh=mesh, in_specs=in_specs, out_specs=out_specs, check_vma=False
    )
```
